128 devices in a mesh: files: 16 (over z, y), clus: 8 (over x, core).
Axes of the slice: x: 4, y: 4, z: 4, core: 2. Of those that a mesh axis runs over, the one named last changes fastest.
Arguments:
- embeddings: bfloat16 [131072, 512], P(('files', 'clus')), may hold values from -192 to 192
- cluster_ids: int32 [131072, 1], P(('files', 'clus')), may hold values from 0 to 63; in each aligned block of 1024 rows (0 to 1023, 1024 to 2047, ...) at most 32 rows name the same one
Outputs:
- earlier_best: float32 [131072], P(('files', 'clus'))
- later_best: float32 [131072], P(('files', 'clus'))
The draws below stay inside these ranges and needn't reach their ends.
Inputs may be any that keep to these rules, and one draw needn't show every extreme that they name: `cluster_ids`: within the rows of one device (aligned blocks of 1024 rows) no cluster is named by more than 32 rows, a bound that some block reaches.
All inputs are finite; a program needn't handle non-finite values.
Results may differ from the reference program's by a relative error of at most 0.00084.
Values may be sent and summed in bfloat16 or wider, within the bound.
A program may use at most 64 MiB of HBM per device.

```python
import math
import jax
import jax.numpy as jnp
import numpy as np
from jax import lax

D = 512
ROW_DEV = 1024
CAP = 32
CLUSTERS = 64
ROWS = 131072
MEMBERS = 4096
PROTOS = 512


def draw_embeddings(key, part):
    key = jax.random.fold_in(key, 11)
    keys = jax.random.split(key, 4)
    directions = jnp.clip(jax.random.normal(keys[0], (PROTOS, D), jnp.float32), -5.0, 5.0)
    picks = jax.random.randint(keys[1], (ROWS,), 0, PROTOS)
    noise = jnp.clip(jax.random.normal(keys[2], (ROWS, D), jnp.float32), -5.0, 5.0)
    weights = jax.random.uniform(keys[3], (ROWS, 1), jnp.float32, 0.3, 1.0)
    return (weights * directions[picks] + noise).astype(jnp.bfloat16)


def routed_block(stream_key, own, number, rows, count, top, limit, skew):
    sequence = jax.random.permutation(stream_key, count)
    crowded, ordinary = load_shares(count, rows * top, limit, skew, True), load_shares(count, rows * top, limit, skew, False)
    places = jnp.arange(count)

    def named(sizes, rotation):
        used = int((sizes > 0).sum())
        fixed = max(1, used // 4)
        shifted = fixed + (places - fixed + rotation * (used - fixed)) % max(1, count - fixed)
        return jnp.zeros((count,), jnp.int32).at[sequence[jnp.where(places < fixed, places, shifted)]].set(jnp.asarray(sizes, jnp.int32))

    sizes = jnp.where(number % 4 == 0, named(crowded, number // 4), named(ordinary, number - number // 4 - 1))
    mixed = jax.random.permutation(jax.random.fold_in(own, 3), count)
    source_of, sink = mixed[0:count // 2 * 2:2], mixed[1:count // 2 * 2:2]
    slack = jnp.minimum(sizes[source_of] - 1, limit - sizes[sink]) // 2
    slack = jnp.where((source_of == sequence[0]) | (sink == sequence[0]) | (sizes[sink] == 0), 0, jnp.maximum(slack, 0))
    shifted = jax.random.randint(jax.random.fold_in(own, 4), (count // 2,), 0, 1 << 20) % (slack + 1)
    sizes = sizes.at[source_of].add(-shifted).at[sink].add(shifted)
    members = jnp.searchsorted(jnp.cumsum(sizes), jnp.arange(rows * top), side="right").astype(jnp.int32)
    grid = members.reshape(top, rows).T
    grid = grid[jax.random.permutation(jax.random.fold_in(own, 1), rows)]
    rotation = jax.random.randint(jax.random.fold_in(own, 2), (rows, 1), 0, top)
    return jnp.take_along_axis(grid, (jnp.arange(top)[None, :] + rotation) % top, axis=1)


def load_shares(number_of, total, bound, lean, full):
    weights = [(1 << 20) // math.isqrt(standing ** lean) + 1 for standing in range(1, number_of + 1)]
    largest = bound if full else min(bound, max(-(-total // number_of), total * weights[0] // sum(weights)))
    least = 1 if total - largest >= number_of - 1 else 0
    given, rest = [largest] + [least] * (number_of - 1), total - largest - least * (number_of - 1)
    while rest > 0:
        candidates = [i for i in range(1, number_of) if given[i] < largest] or [i for i in range(1, number_of) if given[i] < bound]
        whole, left = sum([weights[i] for i in candidates]), rest
        for i in candidates:
            addition = min(bound - given[i], max(1, left * weights[i] // whole), rest)
            given[i] = given[i] + addition
            rest = rest - addition
    return np.array(given)


def setup_inputs(seed: int = 0) -> dict:
    seeds = jax.random.split(jax.random.key(seed), 3)
    embeddings = draw_embeddings(jax.random.fold_in(seeds[2], 71), 0)
    cluster_ids_keys = jax.random.split(jax.random.fold_in(seeds[1], 1), ROWS // ROW_DEV)
    cluster_ids_turns = jax.random.permutation(jax.random.fold_in(seeds[1], 3), ROWS // ROW_DEV)
    cluster_ids = jax.vmap(lambda own, number: routed_block(jax.random.fold_in(seeds[1], 2), own, number, ROW_DEV, CLUSTERS, 1, CAP, 2))(cluster_ids_keys, cluster_ids_turns).reshape((ROWS, 1))
    return dict(embeddings=embeddings, cluster_ids=cluster_ids)


def reference(embeddings, cluster_ids):
    e = embeddings.astype(jnp.float32)
    squares = lax.optimization_barrier(jnp.sum(e * e, axis=1, keepdims=True)) + 1e-06
    unit = (e * lax.rsqrt(squares)).astype(jnp.bfloat16)
    labels = cluster_ids[:, 0].astype(jnp.int32)
    order = jnp.argsort(labels, stable=True).astype(jnp.int32)
    sorted_labels = labels[order]
    counts = lax.optimization_barrier(jnp.sum((labels[None, :] == jnp.arange(CLUSTERS, dtype=jnp.int32)[:, None]).astype(jnp.int32), axis=1))
    starts = (jnp.cumsum(counts) - counts).astype(jnp.int32)
    padded_unit = jnp.concatenate([unit[order], jnp.zeros((MEMBERS, D), jnp.bfloat16)], axis=0)
    padded_rows = jnp.concatenate([order, jnp.full((MEMBERS,), -1, jnp.int32)], axis=0)
    padded_labels = jnp.concatenate([sorted_labels, jnp.full((MEMBERS,), -1, jnp.int32)], axis=0)

    def one_cluster(which):
        begin = starts[which]
        block = lax.dynamic_slice_in_dim(padded_unit, begin, MEMBERS, 0).astype(jnp.float32)
        numbers = lax.dynamic_slice_in_dim(padded_rows, begin, MEMBERS, 0)
        names = lax.dynamic_slice_in_dim(padded_labels, begin, MEMBERS, 0)
        valid = names == which
        similar = jnp.dot(block, block.T, preferred_element_type=jnp.float32)
        both = valid[:, None] & valid[None, :]
        before = both & (numbers[None, :] < numbers[:, None])
        after = both & (numbers[None, :] > numbers[:, None])
        first = lax.optimization_barrier(jnp.max(jnp.where(before, similar, jnp.float32(-1.0)), axis=1))
        second = lax.optimization_barrier(jnp.max(jnp.where(after, similar, jnp.float32(-1.0)), axis=1))
        return (first, second)
    firsts, seconds = lax.map(one_cluster, jnp.arange(CLUSTERS, dtype=jnp.int32))
    position = jnp.arange(ROWS, dtype=jnp.int32) - starts[sorted_labels]
    earlier_best = jnp.zeros((ROWS,), jnp.float32).at[order].set(firsts[sorted_labels, position])
    later_best = jnp.zeros((ROWS,), jnp.float32).at[order].set(seconds[sorted_labels, position])
    return (earlier_best, later_best)
```

```python
import jax
import jax.numpy as jnp
from jax import lax
from jax.experimental import pallas as pl
from jax.experimental.pallas import tpu as pltpu
from jax.sharding import PartitionSpec as P

MESH = pl.DeviceIdType.MESH
SIDE = 4
CHIPS = SIDE**3
CAP = 32
WIDTH = 512
ROWS = 1024
LANES = 128
PHASES = 8
PER = CHIPS // PHASES
BLOCK = PER * CAP
EMPTY = 2.0
NT = (((1,), (1,)), ((), ()))


def kernel(
    emb_ref, lab_ref, first_ref, second_ref,
    raw, unit, outgoing, own, other, acc, bias, res, ret, turned, onehot, rank_s, key_s, count_s,
    raw_sem, self_sem, send_sem, recv_sem, fwd_send, fwd_recv, ret_send, ret_recv,
):
    files, clus = lax.axis_index("files"), lax.axis_index("clus")
    z, y, x, core = files // SIDE, files % SIDE, clus // 2, clus % 2
    chip = (z * SIDE + y) * SIDE + x

    def device(cz, cy, cx, ck):
        return (cz * SIDE + cy, cx * 2 + ck)

    def wrap(v):
        return lax.rem(v + SIDE, SIDE)

    partner = device(z, y, x, 1 - core)
    load = pltpu.make_async_copy(emb_ref, raw, raw_sem)
    load.start()

    barrier = pltpu.get_barrier_semaphore()
    pl.semaphore_signal(barrier, inc=1, device_id=partner, device_id_type=MESH)

    @pl.loop(1, CHIPS)
    def _(i):
        target = device(wrap(z + i // 16), wrap(y + i // 4 % 4), wrap(x + i % 4), core)
        pl.semaphore_signal(barrier, inc=1, device_id=target, device_id_type=MESH)

    labels = lab_ref[...]
    cluster = lax.broadcasted_iota(jnp.int32, (CHIPS, LANES), 0)
    blocks = ROWS // LANES
    hot = [
        jnp.where(labels[:, b * LANES : (b + 1) * LANES] == cluster, 1.0, 0.0) for b in range(blocks)
    ]
    earlier = jnp.where(
        lax.broadcasted_iota(jnp.int32, (LANES, LANES), 0)
        < lax.broadcasted_iota(jnp.int32, (LANES, LANES), 1),
        1.0,
        0.0,
    ).astype(jnp.bfloat16)
    within = jnp.dot(
        jnp.concatenate(hot, axis=0).astype(jnp.bfloat16), earlier, preferred_element_type=jnp.float32
    )
    carry = jnp.zeros((CHIPS, 1), jnp.float32)
    for b in range(blocks):
        lanes = slice(b * LANES, (b + 1) * LANES)
        rank = jnp.sum(
            hot[b] * (within[b * CHIPS : (b + 1) * CHIPS] + carry), axis=0, keepdims=True
        ).astype(jnp.int32)
        rank_s[:, lanes] = rank
        key_s[:, lanes] = labels[:, lanes] * CAP + rank
        onehot[:, lanes] = hot[b].astype(jnp.bfloat16)
        carry = carry + jnp.sum(hot[b], axis=1, keepdims=True)
    count_s[...] = jnp.broadcast_to(carry, (CHIPS, LANES)).astype(jnp.int32)

    load.wait()

    @pl.loop(0, 4)
    def _(i):
        rows = pl.ds(i * (ROWS // 4), ROWS // 4)
        e = raw[rows, :].astype(jnp.float32)
        squares = jnp.sum(e * e, axis=1, keepdims=True) + 1e-06
        unit[rows, :] = (e * lax.rsqrt(squares)).astype(jnp.bfloat16)

    def send(i, stage_x):
        target = device(wrap(z + i // 16), wrap(y + i // 4 % 4), wrap(x + i % 4), core)
        return pltpu.make_async_remote_copy(
            src_ref=outgoing.at[i],
            dst_ref=own.at[stage_x],
            send_sem=send_sem,
            recv_sem=recv_sem.at[i // PER],
            device_id=target,
            device_id_type=MESH,
        )

    keep = pltpu.make_async_copy(outgoing.at[0], own.at[x], self_sem)

    def pack(phase):
        key = key_s[...]
        slot = lax.broadcasted_iota(jnp.int32, (CAP, ROWS), 0)
        picks, holes = [], []
        for j in range(PER):
            i = phase * PER + j
            c = (wrap(z + i // 16) * SIDE + wrap(y + i // 4 % 4)) * SIDE + wrap(x + i % 4)
            picks.append(jnp.where(key - c * CAP == slot, 1.0, 0.0).astype(jnp.bfloat16))
            holes.append(
                (lax.broadcasted_iota(jnp.int32, (CAP, LANES), 0) >= count_s[pl.ds(c, 1), :])
                & (lax.broadcasted_iota(jnp.int32, (CAP, LANES), 1) == 0)
            )
        rows = jnp.dot(jnp.concatenate(picks, axis=0), unit[...], preferred_element_type=jnp.float32)
        for j in range(PER):
            i = phase * PER + j
            part = rows[j * CAP : (j + 1) * CAP]
            outgoing[i, :, :LANES] = jnp.where(holes[j], EMPTY, part[:, :LANES]).astype(jnp.bfloat16)
            outgoing[i, :, LANES:] = part[:, LANES:].astype(jnp.bfloat16)

    pack(0)
    pl.semaphore_wait(barrier, CHIPS)
    keep.start()
    for i in range(1, PER):
        send(i, i // 4 * 4 + x).start()

    @pl.loop(1, PHASES)
    def _(phase):
        pack(phase)
        for j in range(PER):
            i = phase * PER + j
            send(i, i // 4 * 4 + x).start()

    acc[...] = jnp.full(acc.shape, -1.0, jnp.float32)

    def place(phase, half):
        return wrap(z - phase // 2) * SIDE + wrap(y - (phase % 2 * 2 + half))

    def block(ref, phase):
        return ref[pl.ds(phase * PER, PER)].reshape(BLOCK, WIDTH)

    def set_bias(ref, phase, side):
        head = ref[pl.ds(phase * PER, PER), :, pl.ds(0, LANES)].reshape(BLOCK, LANES)
        mark = jnp.transpose(head.astype(jnp.float32))[0:1, :]
        bias[phase * 2 + side] = jnp.where(mark > 1.5, -4.0, 0.0)

    def cross(rows, row_phase, cols, col_phase, side):
        similar = lax.dot_general(rows, cols, NT, preferred_element_type=jnp.float32)
        similar = similar + bias[col_phase * 2 + side]
        for i in range(2):
            for j in range(2):
                after = jnp.where(place(col_phase, j) < place(row_phase, i), 0, 1)
                part = similar[i * LANES : (i + 1) * LANES, j * LANES : (j + 1) * LANES]
                at = pl.ds(pl.multiple_of(row_phase * BLOCK + i * LANES, LANES), LANES)
                acc[after, at, :] = jnp.maximum(acc[after, at, :], part)

    def order(phase, dim, ck):
        r = lax.broadcasted_iota(jnp.int32, (BLOCK, BLOCK), dim)
        group = jnp.where(r < LANES, place(phase, 0), place(phase, 1))
        return group * (2 * LANES) + r % LANES // CAP * (2 * CAP) + ck * CAP + r % CAP

    def diagonal(rows, cols, phase, side):
        similar = lax.dot_general(rows, cols, NT, preferred_element_type=jnp.float32)
        similar = similar + bias[phase * 2 + side]
        mine = order(phase, 0, core)
        theirs = order(phase, 1, jnp.where(side == 0, core, 1 - core))
        at = pl.ds(pl.multiple_of(phase * BLOCK, BLOCK), BLOCK)
        for after in range(2):
            mask = theirs < mine if after == 0 else theirs > mine
            part = jnp.where(mask, similar, -1.0)
            part = jnp.maximum(part[:, :LANES], part[:, LANES:])
            acc[after, at, :] = jnp.maximum(acc[after, at, :], part)

    def forward(phase):
        at = pl.ds(phase * PER, PER)
        return pltpu.make_async_remote_copy(
            src_ref=own.at[at],
            dst_ref=other.at[at],
            send_sem=fwd_send.at[phase],
            recv_sem=fwd_recv.at[phase],
            device_id=partner,
            device_id_type=MESH,
        )

    def arrived(first, number, phase):
        at = pl.ds(first, number)
        pltpu.make_async_remote_copy(
            src_ref=own.at[at],
            dst_ref=own.at[at],
            send_sem=send_sem,
            recv_sem=recv_sem.at[phase],
            device_id=partner,
            device_id_type=MESH,
        ).wait_recv()

    def work(phase):
        forward(phase).start()
        set_bias(own, phase, 0)
        mine = block(own, phase)

        @pl.loop(0, phase)
        def _(u):
            past = block(own, u)
            cross(past, u, mine, phase, 0)
            cross(mine, phase, past, u, 0)
            cross(mine, phase, block(other, u), u, 1)

        diagonal(mine, mine, phase, 0)
        forward(phase).wait_recv()
        set_bias(other, phase, 1)
        theirs = block(other, phase)

        @pl.loop(0, phase)
        def _(u):
            cross(block(own, u), u, theirs, phase, 1)

        diagonal(mine, theirs, phase, 1)

    keep.wait()
    arrived(0, PER - 1, 0)
    work(0)

    @pl.loop(1, PHASES)
    def _(phase):
        arrived(phase * PER, PER, phase)
        work(phase)

    def give(i):
        target = device(wrap(z - i // 16), wrap(y - i // 4 % 4), wrap(x + i % 4), core)
        return pltpu.make_async_remote_copy(
            src_ref=res.at[i // 4],
            dst_ref=ret.at[chip],
            send_sem=ret_send,
            recv_sem=ret_recv,
            device_id=target,
            device_id_type=MESH,
        )

    def finish(stage):
        at = pl.ds(pl.multiple_of(stage * LANES, LANES), LANES)
        for after in range(2):
            best = jnp.max(jnp.transpose(acc[after, at, :]), axis=0, keepdims=True)
            res[stage, after : after + 1, :] = best

    finish(0)
    ret[chip] = res[0]
    for i in range(1, 4):
        give(i).start()

    @pl.loop(1, CHIPS // 4)
    def _(stage):
        finish(stage)
        for j in range(4):
            give(stage * 4 + j).start()

    back = pltpu.make_async_remote_copy(
        src_ref=ret.at[pl.ds(0, CHIPS - 1)],
        dst_ref=ret.at[pl.ds(0, CHIPS - 1)],
        send_sem=ret_send,
        recv_sem=ret_recv,
        device_id=partner,
        device_id_type=MESH,
    )
    back.wait_recv()

    for after in range(2):
        turned[after] = jnp.transpose(ret[:, after, :])
    pieces = []
    for after in range(2):
        rest = turned[after, pl.ds(pl.multiple_of(x * CAP, CAP), CAP), :]
        for _ in range(3):
            piece = rest.astype(jnp.bfloat16)
            pieces.append(piece)
            rest = rest - piece.astype(jnp.float32)
    table = jnp.dot(
        jnp.concatenate(pieces, axis=0), onehot[...], preferred_element_type=jnp.float32
    )
    chosen = lax.broadcasted_iota(jnp.int32, (CAP, ROWS), 0) == rank_s[...]
    for after, out in enumerate((first_ref, second_ref)):
        t = table[after * 3 * CAP : (after + 1) * 3 * CAP]
        value = t[:CAP] + t[CAP : 2 * CAP] + t[2 * CAP :]
        value = jnp.sum(jnp.where(chosen, value, 0.0), axis=0, keepdims=True)
        for b in range(blocks):
            out[b : b + 1, :] = value[:, b * LANES : (b + 1) * LANES]

    back.wait_send()
    pltpu.make_async_remote_copy(
        src_ref=outgoing.at[pl.ds(1, CHIPS - 1)],
        dst_ref=outgoing.at[pl.ds(1, CHIPS - 1)],
        send_sem=send_sem,
        recv_sem=recv_sem.at[0],
        device_id=partner,
        device_id_type=MESH,
    ).wait_send()

    @pl.loop(0, PHASES)
    def _(phase):
        forward(phase).wait_send()


def body(embeddings, cluster_ids):
    vmem = pl.BlockSpec(memory_space=pltpu.VMEM)
    shape = jax.ShapeDtypeStruct((ROWS // LANES, LANES), jnp.float32)
    first, second = pl.pallas_call(
        kernel,
        out_shape=(shape, shape),
        in_specs=[pl.BlockSpec(memory_space=pl.ANY), vmem],
        out_specs=(vmem, vmem),
        scratch_shapes=[
            pltpu.VMEM((ROWS, WIDTH), jnp.bfloat16),
            pltpu.VMEM((ROWS, WIDTH), jnp.bfloat16),
            pltpu.VMEM((CHIPS, CAP, WIDTH), jnp.bfloat16),
            pltpu.VMEM((CHIPS, CAP, WIDTH), jnp.bfloat16),
            pltpu.VMEM((CHIPS, CAP, WIDTH), jnp.bfloat16),
            pltpu.VMEM((2, CHIPS * CAP, LANES), jnp.float32),
            pltpu.VMEM((PHASES * 2, 1, BLOCK), jnp.float32),
            pltpu.VMEM((CHIPS // 4, 2, LANES), jnp.float32),
            pltpu.VMEM((CHIPS, 2, LANES), jnp.float32),
            pltpu.VMEM((2, LANES, CHIPS), jnp.float32),
            pltpu.VMEM((CHIPS, ROWS), jnp.bfloat16),
            pltpu.VMEM((1, ROWS), jnp.int32),
            pltpu.VMEM((1, ROWS), jnp.int32),
            pltpu.VMEM((CHIPS, LANES), jnp.int32),
            pltpu.SemaphoreType.DMA,
            pltpu.SemaphoreType.DMA,
            pltpu.SemaphoreType.DMA,
            pltpu.SemaphoreType.DMA((PHASES,)),
            pltpu.SemaphoreType.DMA((PHASES,)),
            pltpu.SemaphoreType.DMA((PHASES,)),
            pltpu.SemaphoreType.DMA,
            pltpu.SemaphoreType.DMA,
        ],
        compiler_params=pltpu.CompilerParams(
            collective_id=0, has_side_effects=True, vmem_limit_bytes=40 << 20
        ),
        cost_estimate=pl.CostEstimate(
            flops=2 * (2048 * 4096 + 2048 * 1024) * WIDTH, bytes_accessed=2 << 20, transcendentals=ROWS
        ),
    )(embeddings, cluster_ids.reshape(1, ROWS))
    return (first.reshape(ROWS), second.reshape(ROWS))


def solution(mesh):
    placed = (P(("files", "clus"), None), P(("files", "clus"), None))
    return jax.shard_map(
        body,
        mesh=mesh,
        in_specs=placed,
        out_specs=(P(("files", "clus")), P(("files", "clus"))),
        check_vma=False,
    )
```

```python
import jax
import jax.numpy as jnp
from jax import lax
from jax.experimental import pallas as pl
from jax.experimental.pallas import tpu as pltpu
from jax.sharding import PartitionSpec as P

MESH = pl.DeviceIdType.MESH
CHIPS = 64
CAP = 32
WIDTH = 512
ROWS = 1024
LANES = 128
PHASES = 8
PER = CHIPS // PHASES
BLOCK = PER * CAP


def offsets(t, j):
    a = -j % 4
    return (a + t % 4) % 4, (a + 2 * (j // 4) + t // 4) % 4, a


EMPTY = 2.0
NT = (((1,), (1,)), ((), ()))


def kernel(
    emb_ref, lab_ref, out_ref,
    raw, lab, unit, outgoing, own, other, acc, cacc, bias_l, bias_s, masks, orders, res, ret, turned,
    onehot, rank_s, key_s, count_s,
    raw_sem, lab_sem, self_sem, send_sem, recv_sem, fwd_send, fwd_recv, ret_send, ret_recv,
    ring_send, ring_recv,
):
    load = pltpu.make_async_copy(emb_ref, raw, raw_sem)
    load.start()
    load_lab = pltpu.make_async_copy(lab_ref, lab, lab_sem)
    load_lab.start()

    files, clus = lax.axis_index("files"), lax.axis_index("clus")
    z, y = lax.div(files, 4), lax.rem(files, 4)
    x, core = lax.div(clus, 2), lax.rem(clus, 2)
    here = x * 16 + files

    def wrap(v):
        return jnp.where(v >= 4, v - 4, v)

    zs, ys, xs = [[wrap(v + d) for d in range(4)] for v in (z, y, x)]
    partner = (files, clus + 1 - 2 * core)

    def target(t, j):
        dz, dy, dx = offsets(t, j)
        return (zs[dz] * 4 + ys[dy], xs[dx] * 2 + core)

    barrier = pltpu.get_barrier_semaphore()
    for t in range(PHASES):
        for j in range(PER):
            to = target(t, j) if t or j else partner
            pl.semaphore_signal(barrier, inc=1, device_id=to, device_id_type=MESH)

    cluster = lax.broadcasted_iota(jnp.int32, (CHIPS, LANES), 0)
    blocks = ROWS // LANES
    earlier = jnp.where(
        lax.broadcasted_iota(jnp.int32, (LANES, LANES), 0)
        < lax.broadcasted_iota(jnp.int32, (LANES, LANES), 1),
        1.0,
        0.0,
    ).astype(jnp.bfloat16)
    load_lab.wait()
    labels = lab[...]
    labels = labels % 4 * 16 + labels // 4
    hot = [
        jnp.where(labels[:, b * LANES : (b + 1) * LANES] == cluster, 1.0, 0.0) for b in range(blocks)
    ]
    within = jnp.dot(
        jnp.concatenate(hot, axis=0).astype(jnp.bfloat16), earlier, preferred_element_type=jnp.float32
    )
    carry = jnp.zeros((CHIPS, 1), jnp.float32)
    for b in range(blocks):
        lanes = slice(b * LANES, (b + 1) * LANES)
        rank = jnp.sum(
            hot[b] * (within[b * CHIPS : (b + 1) * CHIPS] + carry), axis=0, keepdims=True
        ).astype(jnp.int32)
        rank_s[:, lanes] = rank
        key_s[:, lanes] = labels[:, lanes] * CAP + rank
        onehot[:, lanes] = hot[b].astype(jnp.bfloat16)
        carry = carry + jnp.sum(hot[b], axis=1, keepdims=True)
    count_s[...] = jnp.broadcast_to(carry, (CHIPS, LANES)).astype(jnp.int32)

    load.wait()
    for i in range(4):
        rows = slice(i * (ROWS // 4), (i + 1) * (ROWS // 4))
        e = raw[rows, :].astype(jnp.float32)
        squares = jnp.sum(e * e, axis=1, keepdims=True) + 1e-06
        unit[rows, :] = (e * lax.rsqrt(squares)).astype(jnp.bfloat16)

    def send(t, j):
        return pltpu.make_async_remote_copy(
            src_ref=outgoing.at[t, j],
            dst_ref=own.at[t, j],
            send_sem=send_sem,
            recv_sem=recv_sem.at[t],
            device_id=target(t, j),
            device_id_type=MESH,
        )

    keep = pltpu.make_async_copy(outgoing.at[0, 0], own.at[0, 0], self_sem)

    def pack(t):
        key = key_s[...]
        slot = lax.broadcasted_iota(jnp.int32, (CAP, ROWS), 0)
        row = lax.broadcasted_iota(jnp.int32, (CAP, LANES), 0)
        lane = lax.broadcasted_iota(jnp.int32, (CAP, LANES), 1)
        picks, holes = [], []
        for j in range(PER):
            dz, dy, dx = offsets(t, j)
            c = xs[dx] * 16 + zs[dz] * 4 + ys[dy]
            picks.append(jnp.where(key - c * CAP == slot, 1.0, 0.0).astype(jnp.bfloat16))
            holes.append((row >= count_s[pl.ds(c, 1), :]) & (lane == 0))
        rows = jnp.dot(jnp.concatenate(picks, axis=0), unit[...], preferred_element_type=jnp.float32)
        for j in range(PER):
            part = rows[j * CAP : (j + 1) * CAP]
            outgoing[t, j, :, :LANES] = jnp.where(holes[j], EMPTY, part[:, :LANES]).astype(jnp.bfloat16)
            outgoing[t, j, :, LANES:] = part[:, LANES:].astype(jnp.bfloat16)

    for t in range(PHASES):
        pack(t)
        if t == 0:
            pl.semaphore_wait(barrier, CHIPS)
            keep.start()
        for j in range(PER):
            if t or j:
                send(t, j).start()

    def chip_order(t, j):
        a = -j % 4
        sz = (z - a - t % 4) % 4
        sy = (y - a - 2 * (j // 4) - t // 4) % 4
        return sz * 16 + sy * 4 + (x + j) % 4

    i = lax.broadcasted_iota(jnp.int32, (CHIPS, LANES), 0)
    orders[...] = chip_order(i // PER, i % PER)
    lane_j = lax.broadcasted_iota(jnp.int32, (1, BLOCK), 1) // CAP
    row_i = lax.broadcasted_iota(jnp.int32, (BLOCK, LANES), 0)

    def rows_of(ref, first, last):
        return ref[first:last].reshape((last - first) * BLOCK, WIDTH)

    def product(a, b):
        return lax.dot_general(a, b, NT, preferred_element_type=jnp.float32)

    def set_bias(ref, t, side):
        head = ref[t, :, :, :LANES].reshape(BLOCK, LANES).astype(jnp.float32)
        mark = jnp.broadcast_to(jnp.where(head[:, 0:1] > 1.5, -4.0, 0.0), (BLOCK, LANES))
        bias_s[side, t] = mark
        bias_l[t * 2 + side] = jnp.transpose(mark)[0:1, :]

        if t:
            columns = chip_order(t, lane_j)
            rows = orders[: t * PER, 0:1]
            masks[side, 0, : t * PER, :] = jnp.where(columns < rows, bias_l[t * 2 + side], -4.0)
            masks[side, 1, : t * PER, :] = jnp.where(columns > rows, bias_l[t * 2 + side], -4.0)

    def halves(part):
        return jnp.maximum(part[:, :LANES], part[:, LANES:])

    def maxima(similar, t, side, row_side, rowwise, best):
        for i in range(t * PER):
            u, at = i // PER, slice(i % PER * CAP, (i % PER + 1) * CAP)
            part = similar[i * CAP : (i + 1) * CAP]
            if best is not None:
                mark = bias_s[row_side, u, at, :]
                part = jnp.concatenate([part[:, :LANES] + mark, part[:, LANES:] + mark], axis=1)
            for after in range(2):
                kept = part + masks[side, after, i : i + 1, :]
                if rowwise:
                    acc[after, u, at, :] = jnp.maximum(acc[after, u, at, :], halves(kept))
                if best is not None:
                    high = jnp.max(kept.reshape(CAP // 8, 8, BLOCK), axis=0)
                    best[1 - after] = jnp.maximum(best[1 - after], high)

    def diagonal(t, side):
        similar = product(rows_of(own, t, t + 1), rows_of(other if side else own, t, t + 1))
        similar = similar + bias_l[t * 2 + side]
        lane = lax.broadcasted_iota(jnp.int32, (1, BLOCK), 1)
        mine = (chip_order(t, row_i // CAP) * (2 * CAP) + row_i % CAP)[:, 0:1]
        theirs = chip_order(t, lane_j) * (2 * CAP) + lane % CAP
        if side:
            theirs = theirs + (1 - 2 * core) * CAP
        for after in range(2):
            mask = theirs > mine if after else theirs < mine
            part = halves(jnp.where(mask, similar, -1.0))
            if side:
                acc[after, t] = jnp.maximum(acc[after, t], part)
            else:
                acc[after, t] = jnp.maximum(part, -1.0)

    def forward(t):
        return pltpu.make_async_remote_copy(
            src_ref=own.at[t],
            dst_ref=other.at[t],
            send_sem=fwd_send.at[t],
            recv_sem=fwd_recv.at[t],
            device_id=partner,
            device_id_type=MESH,
        )

    def arrived(t):
        blocks_of = own.at[t] if t else own.at[t, pl.ds(0, PER - 1)]
        pltpu.make_async_remote_copy(
            src_ref=blocks_of,
            dst_ref=blocks_of,
            send_sem=send_sem,
            recv_sem=recv_sem.at[t],
            device_id=partner,
            device_id_type=MESH,
        ).wait_recv()

    for t in range(PHASES):
        if t == 0:
            keep.wait()
        arrived(t)
        forward(t).start()
        set_bias(own, t, 0)
        mine = rows_of(own, t, t + 1)
        best = [jnp.full((8, BLOCK), -1.0, jnp.float32)] * 2
        if t:
            maxima(product(rows_of(own, 0, t), mine), t, 0, 0, True, best)
            maxima(product(rows_of(other, 0, t), mine), t, 0, 1, False, best)
        for after in range(2):
            cacc[t, after] = best[after]
        diagonal(t, 0)
        forward(t).wait_recv()
        set_bias(other, t, 1)
        if t:
            maxima(product(rows_of(own, 0, t), rows_of(other, t, t + 1)), t, 1, 0, True, None)
        diagonal(t, 1)

    quarter = lax.broadcasted_iota(jnp.int32, (1, LANES), 1) // CAP
    lines = {}
    for t in range(PHASES):
        for after in range(2):
            best = jnp.max(jnp.transpose(acc[after, t]), axis=0, keepdims=True)
            best = jnp.maximum(best, jnp.max(cacc[t, after], axis=0, keepdims=True))
            for j in range(PER):
                dz, dy, dx = offsets(t, j)
                line = best[:, j // 4 * LANES : (j // 4 + 1) * LANES]
                key = (dz * 4 + dy, after)
                lines[key] = jnp.where(quarter == j % 4, line, lines[key]) if key in lines else line
    for i in range(16):
        for after in range(2):
            res[i, after : after + 1, :] = pltpu.roll(lines[i, after], x * CAP, 1)
        if i:
            give = pltpu.make_async_remote_copy(
                src_ref=res.at[i],
                dst_ref=ret.at[here],
                send_sem=ret_send,
                recv_sem=ret_recv,
                device_id=(zs[-(i // 4) % 4] * 4 + ys[-(i % 4) % 4], clus),
                device_id_type=MESH,
            )
            give.start()
    ret[here] = res[0]

    def tally(first, number, send_sem, recv_sem):
        return pltpu.make_async_remote_copy(
            src_ref=ret.at[pl.ds(first, number)],
            dst_ref=ret.at[pl.ds(first, number)],
            send_sem=send_sem,
            recv_sem=recv_sem,
            device_id=partner,
            device_id_type=MESH,
        )

    tally(0, 15, ret_send, ret_recv).wait_recv()
    column = ret.at[pl.ds(pl.multiple_of(x * 16, 16), 16)]
    for d in range(1, 4):
        pltpu.make_async_remote_copy(
            src_ref=column,
            dst_ref=column,
            send_sem=ring_send,
            recv_sem=ring_recv,
            device_id=(files, xs[d] * 2 + core),
            device_id_type=MESH,
        ).start()
    tally(0, 48, ring_send, ring_recv).wait_recv()

    for after in range(2):
        turned[after] = jnp.transpose(ret[:, after, :])
    pieces = []
    for after in range(2):
        rest = turned[after, pl.ds(pl.multiple_of(x * CAP, CAP), CAP), :]
        for _ in range(3):
            piece = rest.astype(jnp.bfloat16)
            pieces.append(piece)
            rest = rest - piece.astype(jnp.float32)
    table = jnp.dot(
        jnp.concatenate(pieces, axis=0), onehot[...], preferred_element_type=jnp.float32
    )
    chosen = lax.broadcasted_iota(jnp.int32, (CAP, ROWS), 0) == rank_s[...]
    for after in range(2):
        t = table[after * 3 * CAP : (after + 1) * 3 * CAP]
        value = t[:CAP] + t[CAP : 2 * CAP] + t[2 * CAP :]
        value = jnp.sum(jnp.where(chosen, value, 0.0), axis=0, keepdims=True)
        for b in range(blocks):
            out_ref[after, b : b + 1, :] = value[:, b * LANES : (b + 1) * LANES]

    tally(0, 15, ret_send, ret_recv).wait_send()
    tally(0, 48, ring_send, ring_recv).wait_send()
    sent = pltpu.make_async_remote_copy(
        src_ref=outgoing.at[0, pl.ds(0, PER - 1)],
        dst_ref=outgoing.at[0, pl.ds(0, PER - 1)],
        send_sem=send_sem,
        recv_sem=recv_sem.at[0],
        device_id=partner,
        device_id_type=MESH,
    )
    sent.wait_send()
    pltpu.make_async_remote_copy(
        src_ref=outgoing.at[pl.ds(1, PHASES - 1)],
        dst_ref=outgoing.at[pl.ds(1, PHASES - 1)],
        send_sem=send_sem,
        recv_sem=recv_sem.at[0],
        device_id=partner,
        device_id_type=MESH,
    ).wait_send()
    for t in range(PHASES):
        forward(t).wait_send()


def body(embeddings, cluster_ids):
    anywhere = pl.BlockSpec(memory_space=pl.ANY)
    out = pl.pallas_call(
        kernel,
        out_shape=jax.ShapeDtypeStruct((2, ROWS // LANES, LANES), jnp.float32),
        in_specs=[anywhere, anywhere],
        out_specs=pl.BlockSpec(memory_space=pltpu.VMEM),
        scratch_shapes=[
            pltpu.VMEM((ROWS, WIDTH), jnp.bfloat16),
            pltpu.VMEM((1, ROWS), jnp.int32),
            pltpu.VMEM((ROWS, WIDTH), jnp.bfloat16),
            pltpu.VMEM((PHASES, PER, CAP, WIDTH), jnp.bfloat16),
            pltpu.VMEM((PHASES, PER, CAP, WIDTH), jnp.bfloat16),
            pltpu.VMEM((PHASES, PER, CAP, WIDTH), jnp.bfloat16),
            pltpu.VMEM((2, PHASES, BLOCK, LANES), jnp.float32),
            pltpu.VMEM((PHASES, 2, 8, BLOCK), jnp.float32),
            pltpu.VMEM((PHASES * 2, 1, BLOCK), jnp.float32),
            pltpu.VMEM((2, PHASES, BLOCK, LANES), jnp.float32),
            pltpu.VMEM((2, 2, CHIPS, BLOCK), jnp.float32),
            pltpu.VMEM((CHIPS, LANES), jnp.int32),
            pltpu.VMEM((16, 2, LANES), jnp.float32),
            pltpu.VMEM((CHIPS, 2, LANES), jnp.float32),
            pltpu.VMEM((2, LANES, CHIPS), jnp.float32),
            pltpu.VMEM((CHIPS, ROWS), jnp.bfloat16),
            pltpu.VMEM((1, ROWS), jnp.int32),
            pltpu.VMEM((1, ROWS), jnp.int32),
            pltpu.VMEM((CHIPS, LANES), jnp.int32),
            pltpu.SemaphoreType.DMA,
            pltpu.SemaphoreType.DMA,
            pltpu.SemaphoreType.DMA,
            pltpu.SemaphoreType.DMA,
            pltpu.SemaphoreType.DMA((PHASES,)),
            pltpu.SemaphoreType.DMA((PHASES,)),
            pltpu.SemaphoreType.DMA((PHASES,)),
            pltpu.SemaphoreType.DMA,
            pltpu.SemaphoreType.DMA,
            pltpu.SemaphoreType.DMA,
            pltpu.SemaphoreType.DMA,
        ],
        compiler_params=pltpu.CompilerParams(
            collective_id=0, has_side_effects=True, vmem_limit_bytes=56 << 20
        ),
        cost_estimate=pl.CostEstimate(
            flops=2 * (2048 * 3072 + 2048 * 1024) * WIDTH, bytes_accessed=2 << 20, transcendentals=ROWS
        ),
    )(embeddings, cluster_ids.reshape(1, ROWS))
    return (out[0].reshape(ROWS), out[1].reshape(ROWS))


def solution(mesh):
    placed = (P(("files", "clus"), None), P(("files", "clus"), None))
    return jax.shard_map(
        body,
        mesh=mesh,
        in_specs=placed,
        out_specs=(P(("files", "clus")), P(("files", "clus"))),
        check_vma=False,
    )
```

```python
import jax
import jax.numpy as jnp
from jax import lax
from jax.experimental import pallas as pl
from jax.experimental.pallas import tpu as pltpu
from jax.sharding import PartitionSpec as P

MESH = pl.DeviceIdType.MESH
CHIPS = 64
CAP = 32
WIDTH = 512
ROWS = 1024
LANES = 128
PHASES = 8
PER = CHIPS // PHASES
BLOCK = PER * CAP


def offsets(t, j):
    a = -j % 4
    return (a + t % 4) % 4, (a + 2 * (j // 4) + t // 4) % 4, a


EMPTY = 2.0
NT = (((1,), (1,)), ((), ()))


def hops(offset):
    return sum(min(d, 4 - d) for d in offset)


FAR_FIRST = [sorted(range(PER), key=lambda j: -hops(offsets(t, j))) for t in range(PHASES)]


def kernel(
    emb_ref, lab_ref, out_ref,
    raw, lab, unit, outgoing, own, other, acc, cacc, bias_l, bias_s, masks, orders, res, ret, turned,
    onehot, rank_s, key_s, count_s,
    raw_sem, lab_sem, self_sem, send_sem, recv_sem, fwd_send, fwd_recv, ret_send, ret_recv,
):
    load = pltpu.make_async_copy(emb_ref, raw, raw_sem)
    load.start()
    load_lab = pltpu.make_async_copy(lab_ref, lab, lab_sem)
    load_lab.start()

    files, clus = lax.axis_index("files"), lax.axis_index("clus")
    z, y = lax.div(files, 4), lax.rem(files, 4)
    x, core = lax.div(clus, 2), lax.rem(clus, 2)
    here = x * 16 + files

    def wrap(v):
        return jnp.where(v >= 4, v - 4, v)

    zs, ys, xs = [[wrap(v + d) for d in range(4)] for v in (z, y, x)]
    partner = (files, clus + 1 - 2 * core)

    def target(t, j):
        dz, dy, dx = offsets(t, j)
        return (zs[dz] * 4 + ys[dy], xs[dx] * 2 + core)

    barrier = pltpu.get_barrier_semaphore()
    everyone = [(t, j) for t in range(PHASES) for j in range(PER)]
    for t, j in sorted(everyone, key=lambda tj: -hops(offsets(*tj))):
        to = target(t, j) if t or j else partner
        pl.semaphore_signal(barrier, inc=1, device_id=to, device_id_type=MESH)

    cluster = lax.broadcasted_iota(jnp.int32, (CHIPS, LANES), 0)
    blocks = ROWS // LANES
    earlier = jnp.where(
        lax.broadcasted_iota(jnp.int32, (LANES, LANES), 0)
        < lax.broadcasted_iota(jnp.int32, (LANES, LANES), 1),
        1.0,
        0.0,
    ).astype(jnp.bfloat16)
    load_lab.wait()
    labels = lab[...]
    labels = labels % 4 * 16 + labels // 4
    hot = [
        jnp.where(labels[:, b * LANES : (b + 1) * LANES] == cluster, 1.0, 0.0) for b in range(blocks)
    ]
    within = jnp.dot(
        jnp.concatenate(hot, axis=0).astype(jnp.bfloat16), earlier, preferred_element_type=jnp.float32
    )
    carry = jnp.zeros((CHIPS, 1), jnp.float32)
    for b in range(blocks):
        lanes = slice(b * LANES, (b + 1) * LANES)
        rank = jnp.sum(
            hot[b] * (within[b * CHIPS : (b + 1) * CHIPS] + carry), axis=0, keepdims=True
        ).astype(jnp.int32)
        rank_s[:, lanes] = rank
        key_s[:, lanes] = labels[:, lanes] * CAP + rank
        onehot[:, lanes] = hot[b].astype(jnp.bfloat16)
        carry = carry + jnp.sum(hot[b], axis=1, keepdims=True)
    count_s[...] = jnp.broadcast_to(carry, (CHIPS, LANES)).astype(jnp.int32)

    load.wait()
    for i in range(4):
        rows = slice(i * (ROWS // 4), (i + 1) * (ROWS // 4))
        e = raw[rows, :].astype(jnp.float32)
        squares = jnp.sum(e * e, axis=1, keepdims=True) + 1e-06
        unit[rows, :] = (e * lax.rsqrt(squares)).astype(jnp.bfloat16)

    def send(t, j):
        return pltpu.make_async_remote_copy(
            src_ref=outgoing.at[t, j],
            dst_ref=own.at[t, j],
            send_sem=send_sem,
            recv_sem=recv_sem.at[t],
            device_id=target(t, j),
            device_id_type=MESH,
        )

    keep = pltpu.make_async_copy(outgoing.at[0, 0], own.at[0, 0], self_sem)

    def pack(t):
        key = key_s[...]
        slot = lax.broadcasted_iota(jnp.int32, (CAP, ROWS), 0)
        row = lax.broadcasted_iota(jnp.int32, (CAP, LANES), 0)
        lane = lax.broadcasted_iota(jnp.int32, (CAP, LANES), 1)
        picks, holes = [], []
        for j in range(PER):
            dz, dy, dx = offsets(t, j)
            c = xs[dx] * 16 + zs[dz] * 4 + ys[dy]
            picks.append(jnp.where(key - c * CAP == slot, 1.0, 0.0).astype(jnp.bfloat16))
            holes.append((row >= count_s[pl.ds(c, 1), :]) & (lane == 0))
        rows = jnp.dot(jnp.concatenate(picks, axis=0), unit[...], preferred_element_type=jnp.float32)
        for j in range(PER):
            part = rows[j * CAP : (j + 1) * CAP]
            outgoing[t, j, :, :LANES] = jnp.where(holes[j], EMPTY, part[:, :LANES]).astype(jnp.bfloat16)
            outgoing[t, j, :, LANES:] = part[:, LANES:].astype(jnp.bfloat16)

    for t in range(PHASES):
        pack(t)
        if t == 0:
            pl.semaphore_wait(barrier, CHIPS)
            keep.start()
        for j in FAR_FIRST[t]:
            if t or j:
                send(t, j).start()

    def chip_order(t, j):
        a = -j % 4
        sz = (z - a - t % 4) % 4
        sy = (y - a - 2 * (j // 4) - t // 4) % 4
        return sz * 16 + sy * 4 + (x + j) % 4

    i = lax.broadcasted_iota(jnp.int32, (CHIPS, LANES), 0)
    orders[...] = chip_order(i // PER, i % PER)
    lane_j = lax.broadcasted_iota(jnp.int32, (1, BLOCK), 1) // CAP
    row_i = lax.broadcasted_iota(jnp.int32, (BLOCK, LANES), 0)

    def rows_of(ref, first, last):
        return ref[first:last].reshape((last - first) * BLOCK, WIDTH)

    def product(a, b):
        return lax.dot_general(a, b, NT, preferred_element_type=jnp.float32)

    def set_bias(ref, t, side):
        head = ref[t, :, :, :LANES].reshape(BLOCK, LANES).astype(jnp.float32)
        mark = jnp.broadcast_to(jnp.where(head[:, 0:1] > 1.5, -4.0, 0.0), (BLOCK, LANES))
        bias_s[side, t] = mark
        bias_l[t * 2 + side] = jnp.transpose(mark)[0:1, :]

        if t:
            columns = chip_order(t, lane_j)
            rows = orders[: t * PER, 0:1]
            masks[side, 0, : t * PER, :] = jnp.where(columns < rows, bias_l[t * 2 + side], -4.0)
            masks[side, 1, : t * PER, :] = jnp.where(columns > rows, bias_l[t * 2 + side], -4.0)

    def halves(part):
        return jnp.maximum(part[:, :LANES], part[:, LANES:])

    def maxima(similar, t, side, row_side, rowwise, best):
        for i in range(t * PER):
            u, at = i // PER, slice(i % PER * CAP, (i % PER + 1) * CAP)
            part = similar[i * CAP : (i + 1) * CAP]
            if best is not None:
                mark = bias_s[row_side, u, at, :]
                part = jnp.concatenate([part[:, :LANES] + mark, part[:, LANES:] + mark], axis=1)
            for after in range(2):
                kept = part + masks[side, after, i : i + 1, :]
                if rowwise:
                    acc[after, u, at, :] = jnp.maximum(acc[after, u, at, :], halves(kept))
                if best is not None:
                    high = jnp.max(kept.reshape(CAP // 8, 8, BLOCK), axis=0)
                    best[1 - after] = jnp.maximum(best[1 - after], high)

    def diagonal(t, side):
        similar = product(rows_of(own, t, t + 1), rows_of(other if side else own, t, t + 1))
        similar = similar + bias_l[t * 2 + side]
        lane = lax.broadcasted_iota(jnp.int32, (1, BLOCK), 1)
        mine = (chip_order(t, row_i // CAP) * (2 * CAP) + row_i % CAP)[:, 0:1]
        theirs = chip_order(t, lane_j) * (2 * CAP) + lane % CAP
        if side:
            theirs = theirs + (1 - 2 * core) * CAP
        for after in range(2):
            mask = theirs > mine if after else theirs < mine
            part = halves(jnp.where(mask, similar, -1.0))
            if side:
                acc[after, t] = jnp.maximum(acc[after, t], part)
            else:
                acc[after, t] = jnp.maximum(part, -1.0)

    def forward(t):
        return pltpu.make_async_remote_copy(
            src_ref=own.at[t],
            dst_ref=other.at[t],
            send_sem=fwd_send.at[t],
            recv_sem=fwd_recv.at[t],
            device_id=partner,
            device_id_type=MESH,
        )

    def arrived(t):
        blocks_of = own.at[t] if t else own.at[t, pl.ds(0, PER - 1)]
        pltpu.make_async_remote_copy(
            src_ref=blocks_of,
            dst_ref=blocks_of,
            send_sem=send_sem,
            recv_sem=recv_sem.at[t],
            device_id=partner,
            device_id_type=MESH,
        ).wait_recv()

    for t in range(PHASES):
        if t == 0:
            keep.wait()
        arrived(t)
        forward(t).start()
        set_bias(own, t, 0)
        mine = rows_of(own, t, t + 1)
        best = [jnp.full((8, BLOCK), -1.0, jnp.float32)] * 2
        if t:
            maxima(product(rows_of(own, 0, t), mine), t, 0, 0, True, best)
            maxima(product(rows_of(other, 0, t), mine), t, 0, 1, False, best)
        for after in range(2):
            cacc[t, after] = best[after]
        diagonal(t, 0)
        forward(t).wait_recv()
        set_bias(other, t, 1)
        if t:
            maxima(product(rows_of(own, 0, t), rows_of(other, t, t + 1)), t, 1, 0, True, None)
        diagonal(t, 1)

    quarter = lax.broadcasted_iota(jnp.int32, (1, LANES), 1) // CAP
    lines = {}
    for t in range(PHASES):
        for after in range(2):
            best = jnp.max(jnp.transpose(acc[after, t]), axis=0, keepdims=True)
            best = jnp.maximum(best, jnp.max(cacc[t, after], axis=0, keepdims=True))
            for j in range(PER):
                dz, dy, dx = offsets(t, j)
                line = best[:, j // 4 * LANES : (j // 4 + 1) * LANES]
                key = (dz * 4 + dy, after)
                lines[key] = jnp.where(quarter == j % 4, line, lines[key]) if key in lines else line
    for i in range(16):
        for after in range(2):
            res[i, after : after + 1, :] = pltpu.roll(lines[i, after], x * CAP, 1)
    back = [(dz, dy, dx) for dz in range(4) for dy in range(4) for dx in range(4)]
    for dz, dy, dx in sorted(back, key=hops, reverse=True)[:-1]:
        pltpu.make_async_remote_copy(
            src_ref=res.at[dz * 4 + dy],
            dst_ref=ret.at[here],
            send_sem=ret_send,
            recv_sem=ret_recv,
            device_id=(zs[-dz % 4] * 4 + ys[-dy % 4], xs[-dx % 4] * 2 + core),
            device_id_type=MESH,
        ).start()
    ret[here] = res[0]

    returned = pltpu.make_async_remote_copy(
        src_ref=ret.at[pl.ds(0, CHIPS - 1)],
        dst_ref=ret.at[pl.ds(0, CHIPS - 1)],
        send_sem=ret_send,
        recv_sem=ret_recv,
        device_id=partner,
        device_id_type=MESH,
    )
    returned.wait_recv()

    for after in range(2):
        turned[after] = jnp.transpose(ret[:, after, :])
    pieces = []
    for after in range(2):
        rest = turned[after, pl.ds(pl.multiple_of(x * CAP, CAP), CAP), :]
        for _ in range(3):
            piece = rest.astype(jnp.bfloat16)
            pieces.append(piece)
            rest = rest - piece.astype(jnp.float32)
    table = jnp.dot(
        jnp.concatenate(pieces, axis=0), onehot[...], preferred_element_type=jnp.float32
    )
    chosen = lax.broadcasted_iota(jnp.int32, (CAP, ROWS), 0) == rank_s[...]
    for after in range(2):
        t = table[after * 3 * CAP : (after + 1) * 3 * CAP]
        value = t[:CAP] + t[CAP : 2 * CAP] + t[2 * CAP :]
        value = jnp.sum(jnp.where(chosen, value, 0.0), axis=0, keepdims=True)
        for b in range(blocks):
            out_ref[after, b : b + 1, :] = value[:, b * LANES : (b + 1) * LANES]

    returned.wait_send()
    sent = pltpu.make_async_remote_copy(
        src_ref=outgoing.at[0, pl.ds(0, PER - 1)],
        dst_ref=outgoing.at[0, pl.ds(0, PER - 1)],
        send_sem=send_sem,
        recv_sem=recv_sem.at[0],
        device_id=partner,
        device_id_type=MESH,
    )
    sent.wait_send()
    pltpu.make_async_remote_copy(
        src_ref=outgoing.at[pl.ds(1, PHASES - 1)],
        dst_ref=outgoing.at[pl.ds(1, PHASES - 1)],
        send_sem=send_sem,
        recv_sem=recv_sem.at[0],
        device_id=partner,
        device_id_type=MESH,
    ).wait_send()
    for t in range(PHASES):
        forward(t).wait_send()


def part(both_ref, first_ref, second_ref):
    first_ref[...] = both_ref[0]
    second_ref[...] = both_ref[1]


def body(embeddings, cluster_ids):
    anywhere = pl.BlockSpec(memory_space=pl.ANY)
    out = pl.pallas_call(
        kernel,
        out_shape=jax.ShapeDtypeStruct((2, ROWS // LANES, LANES), jnp.float32),
        in_specs=[anywhere, anywhere],
        out_specs=pl.BlockSpec(memory_space=pltpu.VMEM),
        scratch_shapes=[
            pltpu.VMEM((ROWS, WIDTH), jnp.bfloat16),
            pltpu.VMEM((1, ROWS), jnp.int32),
            pltpu.VMEM((ROWS, WIDTH), jnp.bfloat16),
            pltpu.VMEM((PHASES, PER, CAP, WIDTH), jnp.bfloat16),
            pltpu.VMEM((PHASES, PER, CAP, WIDTH), jnp.bfloat16),
            pltpu.VMEM((PHASES, PER, CAP, WIDTH), jnp.bfloat16),
            pltpu.VMEM((2, PHASES, BLOCK, LANES), jnp.float32),
            pltpu.VMEM((PHASES, 2, 8, BLOCK), jnp.float32),
            pltpu.VMEM((PHASES * 2, 1, BLOCK), jnp.float32),
            pltpu.VMEM((2, PHASES, BLOCK, LANES), jnp.float32),
            pltpu.VMEM((2, 2, CHIPS, BLOCK), jnp.float32),
            pltpu.VMEM((CHIPS, LANES), jnp.int32),
            pltpu.VMEM((16, 2, LANES), jnp.float32),
            pltpu.VMEM((CHIPS, 2, LANES), jnp.float32),
            pltpu.VMEM((2, LANES, CHIPS), jnp.float32),
            pltpu.VMEM((CHIPS, ROWS), jnp.bfloat16),
            pltpu.VMEM((1, ROWS), jnp.int32),
            pltpu.VMEM((1, ROWS), jnp.int32),
            pltpu.VMEM((CHIPS, LANES), jnp.int32),
            pltpu.SemaphoreType.DMA,
            pltpu.SemaphoreType.DMA,
            pltpu.SemaphoreType.DMA,
            pltpu.SemaphoreType.DMA,
            pltpu.SemaphoreType.DMA((PHASES,)),
            pltpu.SemaphoreType.DMA((PHASES,)),
            pltpu.SemaphoreType.DMA((PHASES,)),
            pltpu.SemaphoreType.DMA,
            pltpu.SemaphoreType.DMA,
        ],
        compiler_params=pltpu.CompilerParams(
            collective_id=0, has_side_effects=True, vmem_limit_bytes=56 << 20
        ),
        cost_estimate=pl.CostEstimate(
            flops=2 * (2048 * 3072 + 2048 * 1024) * WIDTH, bytes_accessed=2 << 20, transcendentals=ROWS
        ),
    )(embeddings, cluster_ids.reshape(1, ROWS))
    line = jax.ShapeDtypeStruct((ROWS // LANES, LANES), jnp.float32)
    first, second = pl.pallas_call(
        part,
        out_shape=(line, line),
        in_specs=[pl.BlockSpec(memory_space=pltpu.VMEM)],
        out_specs=[pl.BlockSpec(memory_space=pltpu.VMEM)] * 2,
    )(out)
    return (first.reshape(ROWS), second.reshape(ROWS))


def solution(mesh):
    placed = (P(("files", "clus"), None), P(("files", "clus"), None))
    return jax.shard_map(
        body,
        mesh=mesh,
        in_specs=placed,
        out_specs=(P(("files", "clus")), P(("files", "clus"))),
        check_vma=False,
    )
```

```python
import jax
import jax.numpy as jnp
from jax import lax
from jax.experimental import pallas as pl
from jax.experimental.pallas import tpu as pltpu
from jax.sharding import PartitionSpec as P

MESH = pl.DeviceIdType.MESH
CHIPS = 64
CAP = 32
WIDTH = 512
ROWS = 1024
LANES = 128
PHASES = 8
PER = CHIPS // PHASES
BLOCK = PER * CAP


def offsets(t, j):
    a = -j % 4
    return (a + t % 4) % 4, (a + 2 * (j // 4) + t // 4) % 4, a


EMPTY = 2.0
NT = (((1,), (1,)), ((), ()))


def hops(offset):
    return sum(min(d, 4 - d) for d in offset)


FAR_FIRST = [sorted(range(PER), key=lambda j: -hops(offsets(t, j))) for t in range(PHASES)]


def kernel(
    emb_ref, lab_ref, out_ref,
    raw, lab, unit, outgoing, own, other, acc, cacc, bias_l, bias_s, masks, orders, res, ret, turned,
    onehot, rank_s, key_s, count_s,
    raw_sem, lab_sem, self_sem, send_sem, recv_sem, fwd_send, fwd_recv, ret_send, ret_recv,
):
    load = pltpu.make_async_copy(emb_ref, raw, raw_sem)
    load.start()
    load_lab = pltpu.make_async_copy(lab_ref, lab, lab_sem)
    load_lab.start()

    files, clus = lax.axis_index("files"), lax.axis_index("clus")
    z, y = lax.div(files, 4), lax.rem(files, 4)
    x, core = lax.div(clus, 2), lax.rem(clus, 2)
    here = x * 16 + files

    def wrap(v):
        return jnp.where(v >= 4, v - 4, v)

    zs, ys, xs = [[wrap(v + d) for d in range(4)] for v in (z, y, x)]
    partner = (files, clus + 1 - 2 * core)

    def target(t, j):
        dz, dy, dx = offsets(t, j)
        return (zs[dz] * 4 + ys[dy], xs[dx] * 2 + core)

    barrier = pltpu.get_barrier_semaphore()
    everyone = [(t, j) for t in range(PHASES) for j in range(PER)]
    for t, j in sorted(everyone, key=lambda tj: -hops(offsets(*tj))):
        to = target(t, j) if t or j else partner
        pl.semaphore_signal(barrier, inc=1, device_id=to, device_id_type=MESH)

    cluster = lax.broadcasted_iota(jnp.int32, (CHIPS, LANES), 0)
    blocks = ROWS // LANES
    earlier = jnp.where(
        lax.broadcasted_iota(jnp.int32, (LANES, LANES), 0)
        < lax.broadcasted_iota(jnp.int32, (LANES, LANES), 1),
        1.0,
        0.0,
    ).astype(jnp.bfloat16)
    load_lab.wait()
    labels = lab[...]
    labels = labels % 4 * 16 + labels // 4
    hot = [
        jnp.where(labels[:, b * LANES : (b + 1) * LANES] == cluster, 1.0, 0.0) for b in range(blocks)
    ]
    within = jnp.dot(
        jnp.concatenate(hot, axis=0).astype(jnp.bfloat16), earlier, preferred_element_type=jnp.float32
    )
    carry = jnp.zeros((CHIPS, 1), jnp.float32)
    for b in range(blocks):
        lanes = slice(b * LANES, (b + 1) * LANES)
        rank = jnp.sum(
            hot[b] * (within[b * CHIPS : (b + 1) * CHIPS] + carry), axis=0, keepdims=True
        ).astype(jnp.int32)
        rank_s[:, lanes] = rank
        key_s[:, lanes] = labels[:, lanes] * CAP + rank
        onehot[:, lanes] = hot[b].astype(jnp.bfloat16)
        carry = carry + jnp.sum(hot[b], axis=1, keepdims=True)
    count_s[...] = jnp.broadcast_to(carry, (CHIPS, LANES)).astype(jnp.int32)

    load.wait()
    for i in range(4):
        rows = slice(i * (ROWS // 4), (i + 1) * (ROWS // 4))
        e = raw[rows, :].astype(jnp.float32)
        squares = jnp.sum(e * e, axis=1, keepdims=True) + 1e-06
        unit[rows, :] = (e * lax.rsqrt(squares)).astype(jnp.bfloat16)

    def send(t, j):
        return pltpu.make_async_remote_copy(
            src_ref=outgoing.at[t, j],
            dst_ref=own.at[t, j],
            send_sem=send_sem,
            recv_sem=recv_sem.at[t],
            device_id=target(t, j),
            device_id_type=MESH,
        )

    keep = pltpu.make_async_copy(outgoing.at[0, 0], own.at[0, 0], self_sem)

    def pack(t):
        key = key_s[...]
        slot = lax.broadcasted_iota(jnp.int32, (CAP, ROWS), 0)
        row = lax.broadcasted_iota(jnp.int32, (CAP, LANES), 0)
        lane = lax.broadcasted_iota(jnp.int32, (CAP, LANES), 1)
        picks, holes = [], []
        for j in range(PER):
            dz, dy, dx = offsets(t, j)
            c = xs[dx] * 16 + zs[dz] * 4 + ys[dy]
            picks.append(jnp.where(key - c * CAP == slot, 1.0, 0.0).astype(jnp.bfloat16))
            holes.append((row >= count_s[pl.ds(c, 1), :]) & (lane == 0))
        rows = jnp.dot(jnp.concatenate(picks, axis=0), unit[...], preferred_element_type=jnp.float32)
        for j in range(PER):
            part = rows[j * CAP : (j + 1) * CAP]
            outgoing[t, j, :, :LANES] = jnp.where(holes[j], EMPTY, part[:, :LANES]).astype(jnp.bfloat16)
            outgoing[t, j, :, LANES:] = part[:, LANES:].astype(jnp.bfloat16)

    for t in range(PHASES):
        pack(t)
        if t == 0:
            pl.semaphore_wait(barrier, CHIPS)
            keep.start()
        for j in FAR_FIRST[t]:
            if t or j:
                send(t, j).start()

    def chip_order(t, j):
        a = -j % 4
        sz = (z - a - t % 4) % 4
        sy = (y - a - 2 * (j // 4) - t // 4) % 4
        return sz * 16 + sy * 4 + (x + j) % 4

    i = lax.broadcasted_iota(jnp.int32, (CHIPS, LANES), 0)
    orders[...] = chip_order(i // PER, i % PER)
    lane_j = lax.broadcasted_iota(jnp.int32, (1, BLOCK), 1) // CAP
    row_i = lax.broadcasted_iota(jnp.int32, (BLOCK, LANES), 0)

    def rows_of(ref, first, last):
        return ref[first:last].reshape((last - first) * BLOCK, WIDTH)

    def product(a, b):
        return lax.dot_general(a, b, NT, preferred_element_type=jnp.float32)

    def set_bias(ref, t, side):
        head = ref[t, :, :, :LANES].reshape(BLOCK, LANES).astype(jnp.float32)
        mark = jnp.broadcast_to(jnp.where(head[:, 0:1] > 1.5, -4.0, 0.0), (BLOCK, LANES))
        bias_s[side, t] = mark
        bias_l[t * 2 + side] = jnp.transpose(mark)[0:1, :]

        if t:
            columns = chip_order(t, lane_j)
            rows = orders[: t * PER, 0:1]
            masks[side, 0, : t * PER, :] = jnp.where(columns < rows, bias_l[t * 2 + side], -4.0)
            masks[side, 1, : t * PER, :] = jnp.where(columns > rows, bias_l[t * 2 + side], -4.0)

    def halves(part):
        return jnp.maximum(part[:, :LANES], part[:, LANES:])

    def maxima(similar, t, side, row_side, rowwise, best):
        for i in range(t * PER):
            u, at = i // PER, slice(i % PER * CAP, (i % PER + 1) * CAP)
            part = similar[i * CAP : (i + 1) * CAP]
            if best is not None:
                mark = bias_s[row_side, u, at, :]
                part = jnp.concatenate([part[:, :LANES] + mark, part[:, LANES:] + mark], axis=1)
            for after in range(2):
                kept = part + masks[side, after, i : i + 1, :]
                if rowwise:
                    acc[after, u, at, :] = jnp.maximum(acc[after, u, at, :], halves(kept))
                if best is not None:
                    high = jnp.max(kept.reshape(CAP // 8, 8, BLOCK), axis=0)
                    best[1 - after] = jnp.maximum(best[1 - after], high)

    def diagonal(t, side):
        similar = product(rows_of(own, t, t + 1), rows_of(other if side else own, t, t + 1))
        similar = similar + bias_l[t * 2 + side]
        lane = lax.broadcasted_iota(jnp.int32, (1, BLOCK), 1)
        mine = (chip_order(t, row_i // CAP) * (2 * CAP) + row_i % CAP)[:, 0:1]
        theirs = chip_order(t, lane_j) * (2 * CAP) + lane % CAP
        if side:
            theirs = theirs + (1 - 2 * core) * CAP
        for after in range(2):
            mask = theirs > mine if after else theirs < mine
            part = halves(jnp.where(mask, similar, -1.0))
            if side:
                acc[after, t] = jnp.maximum(acc[after, t], part)
            else:
                acc[after, t] = jnp.maximum(part, -1.0)

    def forward(t):
        return pltpu.make_async_remote_copy(
            src_ref=own.at[t],
            dst_ref=other.at[t],
            send_sem=fwd_send.at[t],
            recv_sem=fwd_recv.at[t],
            device_id=partner,
            device_id_type=MESH,
        )

    def arrived(t):
        blocks_of = own.at[t] if t else own.at[t, pl.ds(0, PER - 1)]
        pltpu.make_async_remote_copy(
            src_ref=blocks_of,
            dst_ref=blocks_of,
            send_sem=send_sem,
            recv_sem=recv_sem.at[t],
            device_id=partner,
            device_id_type=MESH,
        ).wait_recv()

    for t in range(PHASES):
        if t == 0:
            keep.wait()
        arrived(t)
        forward(t).start()
        set_bias(own, t, 0)
        mine = rows_of(own, t, t + 1)
        best = [jnp.full((8, BLOCK), -1.0, jnp.float32)] * 2
        if t:
            maxima(product(rows_of(own, 0, t), mine), t, 0, 0, True, best)
            maxima(product(rows_of(other, 0, t), mine), t, 0, 1, False, best)
        for after in range(2):
            cacc[t, after] = best[after]
        diagonal(t, 0)
        forward(t).wait_recv()
        set_bias(other, t, 1)
        if t:
            maxima(product(rows_of(own, 0, t), rows_of(other, t, t + 1)), t, 1, 0, True, None)
        diagonal(t, 1)

    quarter = lax.broadcasted_iota(jnp.int32, (1, LANES), 1) // CAP
    lines = {}
    for t in range(PHASES):
        for after in range(2):
            best = jnp.max(jnp.transpose(acc[after, t]), axis=0, keepdims=True)
            best = jnp.maximum(best, jnp.max(cacc[t, after], axis=0, keepdims=True))
            for j in range(PER):
                dz, dy, dx = offsets(t, j)
                line = best[:, j // 4 * LANES : (j // 4 + 1) * LANES]
                key = (dz * 4 + dy, after)
                lines[key] = jnp.where(quarter == j % 4, line, lines[key]) if key in lines else line
    for i in range(16):
        for after in range(2):
            res[i, after : after + 1, :] = pltpu.roll(lines[i, after], x * CAP, 1)
    back = [(dz, dy, dx) for dz in range(4) for dy in range(4) for dx in range(4)]
    for dz, dy, dx in sorted(back, key=hops, reverse=True)[:-1]:
        pltpu.make_async_remote_copy(
            src_ref=res.at[dz * 4 + dy],
            dst_ref=ret.at[here],
            send_sem=ret_send,
            recv_sem=ret_recv,
            device_id=(zs[-dz % 4] * 4 + ys[-dy % 4], xs[-dx % 4] * 2 + core),
            device_id_type=MESH,
        ).start()
    ret[here] = res[0]

    returned = pltpu.make_async_remote_copy(
        src_ref=ret.at[pl.ds(0, CHIPS - 1)],
        dst_ref=ret.at[pl.ds(0, CHIPS - 1)],
        send_sem=ret_send,
        recv_sem=ret_recv,
        device_id=partner,
        device_id_type=MESH,
    )
    returned.wait_recv()

    for after in range(2):
        turned[after] = jnp.transpose(ret[:, after, :])
    pieces = []
    for after in range(2):
        rest = turned[after, pl.ds(pl.multiple_of(x * CAP, CAP), CAP), :]
        for _ in range(3):
            piece = rest.astype(jnp.bfloat16)
            pieces.append(piece)
            rest = rest - piece.astype(jnp.float32)
    table = jnp.dot(
        jnp.concatenate(pieces, axis=0), onehot[...], preferred_element_type=jnp.float32
    )
    chosen = lax.broadcasted_iota(jnp.int32, (CAP, ROWS), 0) == rank_s[...]
    for after in range(2):
        t = table[after * 3 * CAP : (after + 1) * 3 * CAP]
        value = t[:CAP] + t[CAP : 2 * CAP] + t[2 * CAP :]
        value = jnp.sum(jnp.where(chosen, value, 0.0), axis=0, keepdims=True)
        for b in range(blocks):
            out_ref[after, b : b + 1, :] = value[:, b * LANES : (b + 1) * LANES]

    returned.wait_send()
    sent = pltpu.make_async_remote_copy(
        src_ref=outgoing.at[0, pl.ds(0, PER - 1)],
        dst_ref=outgoing.at[0, pl.ds(0, PER - 1)],
        send_sem=send_sem,
        recv_sem=recv_sem.at[0],
        device_id=partner,
        device_id_type=MESH,
    )
    sent.wait_send()
    pltpu.make_async_remote_copy(
        src_ref=outgoing.at[pl.ds(1, PHASES - 1)],
        dst_ref=outgoing.at[pl.ds(1, PHASES - 1)],
        send_sem=send_sem,
        recv_sem=recv_sem.at[0],
        device_id=partner,
        device_id_type=MESH,
    ).wait_send()
    for t in range(PHASES):
        forward(t).wait_send()


def part(both_ref, first_ref, second_ref):
    first_ref[...] = both_ref[0]
    second_ref[...] = both_ref[1]


def body(embeddings, cluster_ids):
    anywhere = pl.BlockSpec(memory_space=pl.ANY)
    out = pl.pallas_call(
        kernel,
        out_shape=pltpu.VMEM((2, ROWS // LANES, LANES), jnp.float32),
        in_specs=[anywhere, anywhere],
        out_specs=pl.BlockSpec(memory_space=pltpu.VMEM),
        scratch_shapes=[
            pltpu.VMEM((ROWS, WIDTH), jnp.bfloat16),
            pltpu.VMEM((1, ROWS), jnp.int32),
            pltpu.VMEM((ROWS, WIDTH), jnp.bfloat16),
            pltpu.VMEM((PHASES, PER, CAP, WIDTH), jnp.bfloat16),
            pltpu.VMEM((PHASES, PER, CAP, WIDTH), jnp.bfloat16),
            pltpu.VMEM((PHASES, PER, CAP, WIDTH), jnp.bfloat16),
            pltpu.VMEM((2, PHASES, BLOCK, LANES), jnp.float32),
            pltpu.VMEM((PHASES, 2, 8, BLOCK), jnp.float32),
            pltpu.VMEM((PHASES * 2, 1, BLOCK), jnp.float32),
            pltpu.VMEM((2, PHASES, BLOCK, LANES), jnp.float32),
            pltpu.VMEM((2, 2, CHIPS, BLOCK), jnp.float32),
            pltpu.VMEM((CHIPS, LANES), jnp.int32),
            pltpu.VMEM((16, 2, LANES), jnp.float32),
            pltpu.VMEM((CHIPS, 2, LANES), jnp.float32),
            pltpu.VMEM((2, LANES, CHIPS), jnp.float32),
            pltpu.VMEM((CHIPS, ROWS), jnp.bfloat16),
            pltpu.VMEM((1, ROWS), jnp.int32),
            pltpu.VMEM((1, ROWS), jnp.int32),
            pltpu.VMEM((CHIPS, LANES), jnp.int32),
            pltpu.SemaphoreType.DMA,
            pltpu.SemaphoreType.DMA,
            pltpu.SemaphoreType.DMA,
            pltpu.SemaphoreType.DMA,
            pltpu.SemaphoreType.DMA((PHASES,)),
            pltpu.SemaphoreType.DMA((PHASES,)),
            pltpu.SemaphoreType.DMA((PHASES,)),
            pltpu.SemaphoreType.DMA,
            pltpu.SemaphoreType.DMA,
        ],
        compiler_params=pltpu.CompilerParams(
            collective_id=0, has_side_effects=True, vmem_limit_bytes=56 << 20
        ),
        cost_estimate=pl.CostEstimate(
            flops=2 * (2048 * 3072 + 2048 * 1024) * WIDTH, bytes_accessed=2 << 20, transcendentals=ROWS
        ),
    )(embeddings, cluster_ids.reshape(1, ROWS))
    line = jax.ShapeDtypeStruct((ROWS // LANES, LANES), jnp.float32)
    first, second = pl.pallas_call(
        part,
        out_shape=(line, line),
        in_specs=[pl.BlockSpec(memory_space=pltpu.VMEM)],
        out_specs=[pl.BlockSpec(memory_space=pltpu.VMEM)] * 2,
    )(pltpu.with_memory_space_constraint(out, pltpu.VMEM))
    return (first.reshape(ROWS), second.reshape(ROWS))


def solution(mesh):
    placed = (P(("files", "clus"), None), P(("files", "clus"), None))
    return jax.shard_map(
        body,
        mesh=mesh,
        in_specs=placed,
        out_specs=(P(("files", "clus")), P(("files", "clus"))),
        check_vma=False,
    )
```

```python
import jax
import jax.numpy as jnp
from jax import lax
from jax.experimental import pallas as pl
from jax.experimental.pallas import tpu as pltpu
from jax.sharding import PartitionSpec as P

MESH = pl.DeviceIdType.MESH
CHIPS = 64
CAP = 32
WIDTH = 512
ROWS = 1024
LANES = 128
PHASES = 8
PER = CHIPS // PHASES
BLOCK = PER * CAP


COSETS = (0, 7, 6, 5, 4, 3, 2, 1)


def offsets(t, j):
    a = -j % 4
    coset = COSETS[t]
    return (a + coset % 4) % 4, (a + 2 * (j // 4) + coset // 4) % 4, a


EMPTY = 2.0
NT = (((1,), (1,)), ((), ()))


def hops(offset):
    return sum(min(d, 4 - d) for d in offset)


FAR_FIRST = [sorted(range(PER), key=lambda j: -hops(offsets(t, j))) for t in range(PHASES)]


def kernel(
    emb_ref, lab_ref, out_ref,
    raw, lab, unit, outgoing, own, other, acc, cacc, bias_l, bias_s, masks, orders, res, ret, turned,
    onehot, rank_s, key_s, count_s,
    raw_sem, lab_sem, self_sem, send_sem, recv_sem, fwd_send, fwd_recv, ret_send, ret_recv,
):
    load = pltpu.make_async_copy(emb_ref, raw, raw_sem)
    load.start()
    load_lab = pltpu.make_async_copy(lab_ref, lab, lab_sem)
    load_lab.start()

    files, clus = lax.axis_index("files"), lax.axis_index("clus")
    z, y = lax.div(files, 4), lax.rem(files, 4)
    x, core = lax.div(clus, 2), lax.rem(clus, 2)
    here = x * 16 + files

    def wrap(v):
        return jnp.where(v >= 4, v - 4, v)

    zs, ys, xs = [[wrap(v + d) for d in range(4)] for v in (z, y, x)]
    partner = (files, clus + 1 - 2 * core)

    def target(t, j):
        dz, dy, dx = offsets(t, j)
        return (zs[dz] * 4 + ys[dy], xs[dx] * 2 + core)

    barrier = pltpu.get_barrier_semaphore()
    everyone = [(t, j) for t in range(PHASES) for j in range(PER)]
    for t, j in sorted(everyone, key=lambda tj: -hops(offsets(*tj))):
        to = target(t, j) if t or j else partner
        pl.semaphore_signal(barrier, inc=1, device_id=to, device_id_type=MESH)

    cluster = lax.broadcasted_iota(jnp.int32, (CHIPS, LANES), 0)
    blocks = ROWS // LANES
    earlier = jnp.where(
        lax.broadcasted_iota(jnp.int32, (LANES, LANES), 0)
        < lax.broadcasted_iota(jnp.int32, (LANES, LANES), 1),
        1.0,
        0.0,
    ).astype(jnp.bfloat16)
    load_lab.wait()
    labels = lab[...]
    labels = labels % 4 * 16 + labels // 4
    hot = [
        jnp.where(labels[:, b * LANES : (b + 1) * LANES] == cluster, 1.0, 0.0) for b in range(blocks)
    ]
    within = jnp.dot(
        jnp.concatenate(hot, axis=0).astype(jnp.bfloat16), earlier, preferred_element_type=jnp.float32
    )
    carry = jnp.zeros((CHIPS, 1), jnp.float32)
    for b in range(blocks):
        lanes = slice(b * LANES, (b + 1) * LANES)
        rank = jnp.sum(
            hot[b] * (within[b * CHIPS : (b + 1) * CHIPS] + carry), axis=0, keepdims=True
        ).astype(jnp.int32)
        rank_s[:, lanes] = rank
        key_s[:, lanes] = labels[:, lanes] * CAP + rank
        onehot[:, lanes] = hot[b].astype(jnp.bfloat16)
        carry = carry + jnp.sum(hot[b], axis=1, keepdims=True)
    count_s[...] = jnp.broadcast_to(carry, (CHIPS, LANES)).astype(jnp.int32)

    load.wait()
    for i in range(4):
        rows = slice(i * (ROWS // 4), (i + 1) * (ROWS // 4))
        e = raw[rows, :].astype(jnp.float32)
        squares = jnp.sum(e * e, axis=1, keepdims=True) + 1e-06
        unit[rows, :] = (e * lax.rsqrt(squares)).astype(jnp.bfloat16)

    def send(t, j):
        return pltpu.make_async_remote_copy(
            src_ref=outgoing.at[t, j],
            dst_ref=own.at[t, j],
            send_sem=send_sem,
            recv_sem=recv_sem.at[t],
            device_id=target(t, j),
            device_id_type=MESH,
        )

    keep = pltpu.make_async_copy(outgoing.at[0, 0], own.at[0, 0], self_sem)

    def pack(t):
        key = key_s[...]
        slot = lax.broadcasted_iota(jnp.int32, (CAP, ROWS), 0)
        row = lax.broadcasted_iota(jnp.int32, (CAP, LANES), 0)
        lane = lax.broadcasted_iota(jnp.int32, (CAP, LANES), 1)
        picks, holes = [], []
        for j in range(PER):
            dz, dy, dx = offsets(t, j)
            c = xs[dx] * 16 + zs[dz] * 4 + ys[dy]
            picks.append(jnp.where(key - c * CAP == slot, 1.0, 0.0).astype(jnp.bfloat16))
            holes.append((row >= count_s[pl.ds(c, 1), :]) & (lane == 0))
        rows = jnp.dot(jnp.concatenate(picks, axis=0), unit[...], preferred_element_type=jnp.float32)
        for j in range(PER):
            part = rows[j * CAP : (j + 1) * CAP]
            outgoing[t, j, :, :LANES] = jnp.where(holes[j], EMPTY, part[:, :LANES]).astype(jnp.bfloat16)
            outgoing[t, j, :, LANES:] = part[:, LANES:].astype(jnp.bfloat16)

    for t in range(PHASES):
        pack(t)
        if t == 0:
            pl.semaphore_wait(barrier, CHIPS)
            keep.start()
        for j in FAR_FIRST[t]:
            if t or j:
                send(t, j).start()

    def chip_order(coset, j):
        a = -j % 4
        sz = (z - a - coset % 4) % 4
        sy = (y - a - 2 * (j // 4) - coset // 4) % 4
        return sz * 16 + sy * 4 + (x + j) % 4

    i = lax.broadcasted_iota(jnp.int32, (PER, LANES), 0)
    for t in range(PHASES):
        orders[t * PER : (t + 1) * PER, :] = chip_order(COSETS[t], i)
    lane_j = lax.broadcasted_iota(jnp.int32, (1, BLOCK), 1) // CAP
    row_i = lax.broadcasted_iota(jnp.int32, (BLOCK, LANES), 0)

    def rows_of(ref, first, last):
        return ref[first:last].reshape((last - first) * BLOCK, WIDTH)

    def product(a, b):
        return lax.dot_general(a, b, NT, preferred_element_type=jnp.float32)

    def set_bias(ref, t, side):
        head = ref[t, :, :, :LANES].reshape(BLOCK, LANES).astype(jnp.float32)
        mark = jnp.broadcast_to(jnp.where(head[:, 0:1] > 1.5, -4.0, 0.0), (BLOCK, LANES))
        bias_s[side, t] = mark
        bias_l[t * 2 + side] = jnp.transpose(mark)[0:1, :]

        if t:
            columns = chip_order(COSETS[t], lane_j)
            rows = orders[: t * PER, 0:1]
            masks[side, 0, : t * PER, :] = jnp.where(columns < rows, bias_l[t * 2 + side], -4.0)
            masks[side, 1, : t * PER, :] = jnp.where(columns > rows, bias_l[t * 2 + side], -4.0)

    def halves(part):
        return jnp.maximum(part[:, :LANES], part[:, LANES:])

    def maxima(similar, t, side, row_side, rowwise, best):
        for i in range(t * PER):
            u, at = i // PER, slice(i % PER * CAP, (i % PER + 1) * CAP)
            part = similar[i * CAP : (i + 1) * CAP]
            if best is not None:
                mark = bias_s[row_side, u, at, :]
                part = jnp.concatenate([part[:, :LANES] + mark, part[:, LANES:] + mark], axis=1)
            for after in range(2):
                kept = part + masks[side, after, i : i + 1, :]
                if rowwise:
                    acc[after, u, at, :] = jnp.maximum(acc[after, u, at, :], halves(kept))
                if best is not None:
                    high = jnp.max(kept.reshape(CAP // 8, 8, BLOCK), axis=0)
                    best[1 - after] = jnp.maximum(best[1 - after], high)

    def diagonal(t, side):
        similar = product(rows_of(own, t, t + 1), rows_of(other if side else own, t, t + 1))
        similar = similar + bias_l[t * 2 + side]
        lane = lax.broadcasted_iota(jnp.int32, (1, BLOCK), 1)
        mine = (chip_order(COSETS[t], row_i // CAP) * (2 * CAP) + row_i % CAP)[:, 0:1]
        theirs = chip_order(COSETS[t], lane_j) * (2 * CAP) + lane % CAP
        if side:
            theirs = theirs + (1 - 2 * core) * CAP
        for after in range(2):
            mask = theirs > mine if after else theirs < mine
            part = halves(jnp.where(mask, similar, -1.0))
            if side:
                acc[after, t] = jnp.maximum(acc[after, t], part)
            else:
                acc[after, t] = jnp.maximum(part, -1.0)

    def forward(t):
        return pltpu.make_async_remote_copy(
            src_ref=own.at[t],
            dst_ref=other.at[t],
            send_sem=fwd_send.at[t],
            recv_sem=fwd_recv.at[t],
            device_id=partner,
            device_id_type=MESH,
        )

    def arrived(t):
        blocks_of = own.at[t] if t else own.at[t, pl.ds(0, PER - 1)]
        pltpu.make_async_remote_copy(
            src_ref=blocks_of,
            dst_ref=blocks_of,
            send_sem=send_sem,
            recv_sem=recv_sem.at[t],
            device_id=partner,
            device_id_type=MESH,
        ).wait_recv()

    for t in range(PHASES):
        if t == 0:
            keep.wait()
        arrived(t)
        forward(t).start()
        set_bias(own, t, 0)
        mine = rows_of(own, t, t + 1)
        best = [jnp.full((8, BLOCK), -1.0, jnp.float32)] * 2
        if t:
            maxima(product(rows_of(own, 0, t), mine), t, 0, 0, True, best)
            maxima(product(rows_of(other, 0, t), mine), t, 0, 1, False, best)
        for after in range(2):
            cacc[t, after] = best[after]
        diagonal(t, 0)
        forward(t).wait_recv()
        set_bias(other, t, 1)
        if t:
            maxima(product(rows_of(own, 0, t), rows_of(other, t, t + 1)), t, 1, 0, True, None)
        diagonal(t, 1)

    quarter = lax.broadcasted_iota(jnp.int32, (1, LANES), 1) // CAP
    lines = {}
    for t in range(PHASES):
        for after in range(2):
            best = jnp.max(jnp.transpose(acc[after, t]), axis=0, keepdims=True)
            best = jnp.maximum(best, jnp.max(cacc[t, after], axis=0, keepdims=True))
            for j in range(PER):
                dz, dy, dx = offsets(t, j)
                line = best[:, j // 4 * LANES : (j // 4 + 1) * LANES]
                key = (dz * 4 + dy, after)
                lines[key] = jnp.where(quarter == j % 4, line, lines[key]) if key in lines else line
    for i in range(16):
        for after in range(2):
            res[i, after : after + 1, :] = pltpu.roll(lines[i, after], x * CAP, 1)
    back = [(dz, dy, dx) for dz in range(4) for dy in range(4) for dx in range(4)]
    for dz, dy, dx in sorted(back, key=hops, reverse=True)[:-1]:
        pltpu.make_async_remote_copy(
            src_ref=res.at[dz * 4 + dy],
            dst_ref=ret.at[here],
            send_sem=ret_send,
            recv_sem=ret_recv,
            device_id=(zs[-dz % 4] * 4 + ys[-dy % 4], xs[-dx % 4] * 2 + core),
            device_id_type=MESH,
        ).start()
    ret[here] = res[0]

    returned = pltpu.make_async_remote_copy(
        src_ref=ret.at[pl.ds(0, CHIPS - 1)],
        dst_ref=ret.at[pl.ds(0, CHIPS - 1)],
        send_sem=ret_send,
        recv_sem=ret_recv,
        device_id=partner,
        device_id_type=MESH,
    )
    returned.wait_recv()

    for after in range(2):
        turned[after] = jnp.transpose(ret[:, after, :])
    pieces = []
    for after in range(2):
        rest = turned[after, pl.ds(pl.multiple_of(x * CAP, CAP), CAP), :]
        for _ in range(3):
            piece = rest.astype(jnp.bfloat16)
            pieces.append(piece)
            rest = rest - piece.astype(jnp.float32)
    table = jnp.dot(
        jnp.concatenate(pieces, axis=0), onehot[...], preferred_element_type=jnp.float32
    )
    chosen = lax.broadcasted_iota(jnp.int32, (CAP, ROWS), 0) == rank_s[...]
    for after in range(2):
        t = table[after * 3 * CAP : (after + 1) * 3 * CAP]
        value = t[:CAP] + t[CAP : 2 * CAP] + t[2 * CAP :]
        value = jnp.sum(jnp.where(chosen, value, 0.0), axis=0, keepdims=True)
        for b in range(blocks):
            out_ref[after, b : b + 1, :] = value[:, b * LANES : (b + 1) * LANES]

    returned.wait_send()
    sent = pltpu.make_async_remote_copy(
        src_ref=outgoing.at[0, pl.ds(0, PER - 1)],
        dst_ref=outgoing.at[0, pl.ds(0, PER - 1)],
        send_sem=send_sem,
        recv_sem=recv_sem.at[0],
        device_id=partner,
        device_id_type=MESH,
    )
    sent.wait_send()
    pltpu.make_async_remote_copy(
        src_ref=outgoing.at[pl.ds(1, PHASES - 1)],
        dst_ref=outgoing.at[pl.ds(1, PHASES - 1)],
        send_sem=send_sem,
        recv_sem=recv_sem.at[0],
        device_id=partner,
        device_id_type=MESH,
    ).wait_send()
    for t in range(PHASES):
        forward(t).wait_send()


def part(both_ref, first_ref, second_ref):
    first_ref[...] = both_ref[0]
    second_ref[...] = both_ref[1]


def body(embeddings, cluster_ids):
    anywhere = pl.BlockSpec(memory_space=pl.ANY)
    out = pl.pallas_call(
        kernel,
        out_shape=pltpu.VMEM((2, ROWS // LANES, LANES), jnp.float32),
        in_specs=[anywhere, anywhere],
        out_specs=pl.BlockSpec(memory_space=pltpu.VMEM),
        scratch_shapes=[
            pltpu.VMEM((ROWS, WIDTH), jnp.bfloat16),
            pltpu.VMEM((1, ROWS), jnp.int32),
            pltpu.VMEM((ROWS, WIDTH), jnp.bfloat16),
            pltpu.VMEM((PHASES, PER, CAP, WIDTH), jnp.bfloat16),
            pltpu.VMEM((PHASES, PER, CAP, WIDTH), jnp.bfloat16),
            pltpu.VMEM((PHASES, PER, CAP, WIDTH), jnp.bfloat16),
            pltpu.VMEM((2, PHASES, BLOCK, LANES), jnp.float32),
            pltpu.VMEM((PHASES, 2, 8, BLOCK), jnp.float32),
            pltpu.VMEM((PHASES * 2, 1, BLOCK), jnp.float32),
            pltpu.VMEM((2, PHASES, BLOCK, LANES), jnp.float32),
            pltpu.VMEM((2, 2, CHIPS, BLOCK), jnp.float32),
            pltpu.VMEM((CHIPS, LANES), jnp.int32),
            pltpu.VMEM((16, 2, LANES), jnp.float32),
            pltpu.VMEM((CHIPS, 2, LANES), jnp.float32),
            pltpu.VMEM((2, LANES, CHIPS), jnp.float32),
            pltpu.VMEM((CHIPS, ROWS), jnp.bfloat16),
            pltpu.VMEM((1, ROWS), jnp.int32),
            pltpu.VMEM((1, ROWS), jnp.int32),
            pltpu.VMEM((CHIPS, LANES), jnp.int32),
            pltpu.SemaphoreType.DMA,
            pltpu.SemaphoreType.DMA,
            pltpu.SemaphoreType.DMA,
            pltpu.SemaphoreType.DMA,
            pltpu.SemaphoreType.DMA((PHASES,)),
            pltpu.SemaphoreType.DMA((PHASES,)),
            pltpu.SemaphoreType.DMA((PHASES,)),
            pltpu.SemaphoreType.DMA,
            pltpu.SemaphoreType.DMA,
        ],
        compiler_params=pltpu.CompilerParams(
            collective_id=0, has_side_effects=True, vmem_limit_bytes=56 << 20
        ),
        cost_estimate=pl.CostEstimate(
            flops=2 * (2048 * 3072 + 2048 * 1024) * WIDTH, bytes_accessed=2 << 20, transcendentals=ROWS
        ),
    )(embeddings, cluster_ids.reshape(1, ROWS))
    line = jax.ShapeDtypeStruct((ROWS // LANES, LANES), jnp.float32)
    first, second = pl.pallas_call(
        part,
        out_shape=(line, line),
        in_specs=[pl.BlockSpec(memory_space=pltpu.VMEM)],
        out_specs=[pl.BlockSpec(memory_space=pltpu.VMEM)] * 2,
    )(pltpu.with_memory_space_constraint(out, pltpu.VMEM))
    return (first.reshape(ROWS), second.reshape(ROWS))


def solution(mesh):
    placed = (P(("files", "clus"), None), P(("files", "clus"), None))
    return jax.shard_map(
        body,
        mesh=mesh,
        in_specs=placed,
        out_specs=(P(("files", "clus")), P(("files", "clus"))),
        check_vma=False,
    )
```

```python
import jax
import jax.numpy as jnp
from jax import lax
from jax.experimental import pallas as pl
from jax.experimental.pallas import tpu as pltpu
from jax.sharding import PartitionSpec as P

MESH = pl.DeviceIdType.MESH
CHIPS = 64
CAP = 32
WIDTH = 512
ROWS = 1024
LANES = 128
PHASES = 8
PER = CHIPS // PHASES
BLOCK = PER * CAP


COSETS = (0, 7, 6, 5, 4, 3, 2, 1)


def offsets(t, j):
    a = -j % 4
    coset = COSETS[t]
    return (a + coset % 4) % 4, (a + 2 * (j // 4) + coset // 4) % 4, a


EMPTY = 2.0
NT = (((1,), (1,)), ((), ()))


def hops(offset):
    return sum(min(d, 4 - d) for d in offset)


FAR_FIRST = [sorted(range(PER), key=lambda j: -hops(offsets(t, j))) for t in range(PHASES)]


def kernel(
    emb_ref, lab_ref, out_ref,
    raw, lab, unit, outgoing, own, other, acc, cacc, bias_l, bias_s, masks, orders, res, ret, turned,
    onehot, rank_s, key_s, count_s,
    raw_sem, lab_sem, self_sem, send_sem, recv_sem, fwd_send, fwd_recv, ret_send, ret_recv,
):
    load = pltpu.make_async_copy(emb_ref, raw, raw_sem)
    load.start()
    load_lab = pltpu.make_async_copy(lab_ref, lab, lab_sem)
    load_lab.start()

    files, clus = lax.axis_index("files"), lax.axis_index("clus")
    z, y = lax.div(files, 4), lax.rem(files, 4)
    x, core = lax.div(clus, 2), lax.rem(clus, 2)
    here = x * 16 + files

    def wrap(v):
        return jnp.where(v >= 4, v - 4, v)

    zs, ys, xs = [[wrap(v + d) for d in range(4)] for v in (z, y, x)]
    partner = (files, clus + 1 - 2 * core)

    def target(t, j):
        dz, dy, dx = offsets(t, j)
        return (zs[dz] * 4 + ys[dy], xs[dx] * 2 + core)

    barrier = pltpu.get_barrier_semaphore()
    everyone = [(t, j) for t in range(PHASES) for j in range(PER)]
    for t, j in sorted(everyone, key=lambda tj: -hops(offsets(*tj))):
        to = target(t, j) if t or j else partner
        pl.semaphore_signal(barrier, inc=1, device_id=to, device_id_type=MESH)

    cluster = lax.broadcasted_iota(jnp.int32, (CHIPS, LANES), 0)
    blocks = ROWS // LANES
    earlier = jnp.where(
        lax.broadcasted_iota(jnp.int32, (LANES, LANES), 0)
        < lax.broadcasted_iota(jnp.int32, (LANES, LANES), 1),
        1.0,
        0.0,
    ).astype(jnp.bfloat16)
    load_lab.wait()
    labels = lab[...]
    labels = labels % 4 * 16 + labels // 4
    hot = [
        jnp.where(labels[:, b * LANES : (b + 1) * LANES] == cluster, 1.0, 0.0) for b in range(blocks)
    ]
    within = jnp.dot(
        jnp.concatenate(hot, axis=0).astype(jnp.bfloat16), earlier, preferred_element_type=jnp.float32
    )
    carry = jnp.zeros((CHIPS, 1), jnp.float32)
    for b in range(blocks):
        lanes = slice(b * LANES, (b + 1) * LANES)
        rank = jnp.sum(
            hot[b] * (within[b * CHIPS : (b + 1) * CHIPS] + carry), axis=0, keepdims=True
        ).astype(jnp.int32)
        rank_s[:, lanes] = rank
        key_s[:, lanes] = labels[:, lanes] * CAP + rank
        onehot[:, lanes] = hot[b].astype(jnp.bfloat16)
        carry = carry + jnp.sum(hot[b], axis=1, keepdims=True)
    count_s[...] = jnp.broadcast_to(carry, (CHIPS, LANES)).astype(jnp.int32)

    load.wait()
    for i in range(4):
        rows = slice(i * (ROWS // 4), (i + 1) * (ROWS // 4))
        e = raw[rows, :].astype(jnp.float32)
        squares = jnp.sum(e * e, axis=1, keepdims=True) + 1e-06
        unit[rows, :] = (e * lax.rsqrt(squares)).astype(jnp.bfloat16)

    def send(t, j):
        return pltpu.make_async_remote_copy(
            src_ref=outgoing.at[t, j],
            dst_ref=own.at[t, j],
            send_sem=send_sem,
            recv_sem=recv_sem.at[t],
            device_id=target(t, j),
            device_id_type=MESH,
        )

    keep = pltpu.make_async_copy(outgoing.at[0, 0], own.at[0, 0], self_sem)

    def pack(t):
        key = key_s[...]
        slot = lax.broadcasted_iota(jnp.int32, (CAP, ROWS), 0)
        row = lax.broadcasted_iota(jnp.int32, (CAP, LANES), 0)
        lane = lax.broadcasted_iota(jnp.int32, (CAP, LANES), 1)
        picks, holes = [], []
        for j in range(PER):
            dz, dy, dx = offsets(t, j)
            c = xs[dx] * 16 + zs[dz] * 4 + ys[dy]
            picks.append(jnp.where(key - c * CAP == slot, 1.0, 0.0).astype(jnp.bfloat16))
            holes.append((row >= count_s[pl.ds(c, 1), :]) & (lane == 0))
        rows = jnp.dot(jnp.concatenate(picks, axis=0), unit[...], preferred_element_type=jnp.float32)
        for j in range(PER):
            part = rows[j * CAP : (j + 1) * CAP]
            outgoing[t, j, :, :LANES] = jnp.where(holes[j], EMPTY, part[:, :LANES]).astype(jnp.bfloat16)
            outgoing[t, j, :, LANES:] = part[:, LANES:].astype(jnp.bfloat16)

    for t in range(PHASES):
        pack(t)
        if t == 0:
            pl.semaphore_wait(barrier, CHIPS)
            keep.start()
        for j in FAR_FIRST[t]:
            if t or j:
                send(t, j).start()

    def chip_order(coset, j):
        a = -j % 4
        sz = (z - a - coset % 4) % 4
        sy = (y - a - 2 * (j // 4) - coset // 4) % 4
        return sz * 16 + sy * 4 + (x + j) % 4

    i = lax.broadcasted_iota(jnp.int32, (PER, LANES), 0)
    for t in range(PHASES):
        orders[t * PER : (t + 1) * PER, :] = chip_order(COSETS[t], i)
    lane_j = lax.broadcasted_iota(jnp.int32, (1, BLOCK), 1) // CAP
    row_i = lax.broadcasted_iota(jnp.int32, (BLOCK, LANES), 0)

    def rows_of(ref, first, last):
        return ref[first:last].reshape((last - first) * BLOCK, WIDTH)

    def product(a, b):
        return lax.dot_general(a, b, NT, preferred_element_type=jnp.float32)

    def set_bias(ref, t, side):
        head = ref[t, :, :, :LANES].reshape(BLOCK, LANES).astype(jnp.float32)
        mark = jnp.broadcast_to(jnp.where(head[:, 0:1] > 1.5, -4.0, 0.0), (BLOCK, LANES))
        bias_s[side, t] = mark
        bias_l[t * 2 + side] = jnp.transpose(mark)[0:1, :]

        if t:
            columns = chip_order(COSETS[t], lane_j)
            rows = orders[: t * PER, 0:1]
            masks[side, 0, : t * PER, :] = jnp.where(columns < rows, bias_l[t * 2 + side], -4.0)
            masks[side, 1, : t * PER, :] = jnp.where(columns > rows, bias_l[t * 2 + side], -4.0)

    def halves(part):
        return jnp.maximum(part[:, :LANES], part[:, LANES:])

    def maxima(similar, t, side, row_side, rowwise, best):
        for i in range(t * PER):
            u, at = i // PER, slice(i % PER * CAP, (i % PER + 1) * CAP)
            part = similar[i * CAP : (i + 1) * CAP]
            if best is not None:
                mark = bias_s[row_side, u, at, :]
                part = jnp.concatenate([part[:, :LANES] + mark, part[:, LANES:] + mark], axis=1)
            for after in range(2):
                kept = part + masks[side, after, i : i + 1, :]
                if rowwise:
                    acc[after, u, at, :] = jnp.maximum(acc[after, u, at, :], halves(kept))
                if best is not None:
                    high = jnp.max(kept.reshape(CAP // 8, 8, BLOCK), axis=0)
                    best[1 - after] = jnp.maximum(best[1 - after], high)

    def diagonal(t, side):
        similar = product(rows_of(own, t, t + 1), rows_of(other if side else own, t, t + 1))
        similar = similar + bias_l[t * 2 + side]
        lane = lax.broadcasted_iota(jnp.int32, (1, BLOCK), 1)
        mine = (chip_order(COSETS[t], row_i // CAP) * (2 * CAP) + row_i % CAP)[:, 0:1]
        theirs = chip_order(COSETS[t], lane_j) * (2 * CAP) + lane % CAP
        if side:
            theirs = theirs + (1 - 2 * core) * CAP
        for after in range(2):
            mask = theirs > mine if after else theirs < mine
            part = halves(jnp.where(mask, similar, -1.0))
            if side:
                acc[after, t] = jnp.maximum(acc[after, t], part)
            else:
                acc[after, t] = jnp.maximum(part, -1.0)

    def forward(t):
        return pltpu.make_async_remote_copy(
            src_ref=own.at[t],
            dst_ref=other.at[t],
            send_sem=fwd_send.at[t],
            recv_sem=fwd_recv.at[t],
            device_id=partner,
            device_id_type=MESH,
        )

    def arrived(t):
        blocks_of = own.at[t] if t else own.at[t, pl.ds(0, PER - 1)]
        pltpu.make_async_remote_copy(
            src_ref=blocks_of,
            dst_ref=blocks_of,
            send_sem=send_sem,
            recv_sem=recv_sem.at[t],
            device_id=partner,
            device_id_type=MESH,
        ).wait_recv()

    for t in range(PHASES):
        if t == 0:
            keep.wait()
        arrived(t)
        forward(t).start()
        set_bias(own, t, 0)
        mine = rows_of(own, t, t + 1)
        best = [jnp.full((8, BLOCK), -1.0, jnp.float32)] * 2
        if t:
            maxima(product(rows_of(own, 0, t), mine), t, 0, 0, True, best)
            maxima(product(rows_of(other, 0, t), mine), t, 0, 1, False, best)
        for after in range(2):
            cacc[t, after] = best[after]
        diagonal(t, 0)
        forward(t).wait_recv()
        set_bias(other, t, 1)
        if t:
            maxima(product(rows_of(own, 0, t), rows_of(other, t, t + 1)), t, 1, 0, True, None)
        diagonal(t, 1)

    for t in range(PHASES):
        for after in range(2):
            best = jnp.max(jnp.transpose(acc[after, t]), axis=0, keepdims=True)
            best = jnp.maximum(best, jnp.max(cacc[t, after], axis=0, keepdims=True))
            for half in range(2):
                line = best[:, half * LANES : (half + 1) * LANES]
                res[t * 2 + half, after : after + 1, :] = pltpu.roll(line, x * CAP, 1)
    line_of = {offsets(t, j): t * 2 + j // 4 for t in range(PHASES) for j in range(PER)}
    back = [(dz, dy, dx) for dz in range(4) for dy in range(4) for dx in range(4)]
    for dz, dy, dx in sorted(back, key=hops, reverse=True)[:-1]:
        pltpu.make_async_remote_copy(
            src_ref=res.at[line_of[dz, dy, dx]],
            dst_ref=ret.at[here],
            send_sem=ret_send,
            recv_sem=ret_recv,
            device_id=(zs[-dz % 4] * 4 + ys[-dy % 4], xs[-dx % 4] * 2 + core),
            device_id_type=MESH,
        ).start()
    ret[here] = res[0]

    returned = pltpu.make_async_remote_copy(
        src_ref=ret.at[pl.ds(0, CHIPS - 1)],
        dst_ref=ret.at[pl.ds(0, CHIPS - 1)],
        send_sem=ret_send,
        recv_sem=ret_recv,
        device_id=partner,
        device_id_type=MESH,
    )
    returned.wait_recv()

    for after in range(2):
        turned[after] = jnp.transpose(ret[:, after, :])
    pieces = []
    for after in range(2):
        rest = turned[after, pl.ds(pl.multiple_of(x * CAP, CAP), CAP), :]
        for _ in range(3):
            piece = rest.astype(jnp.bfloat16)
            pieces.append(piece)
            rest = rest - piece.astype(jnp.float32)
    table = jnp.dot(
        jnp.concatenate(pieces, axis=0), onehot[...], preferred_element_type=jnp.float32
    )
    chosen = lax.broadcasted_iota(jnp.int32, (CAP, ROWS), 0) == rank_s[...]
    for after in range(2):
        t = table[after * 3 * CAP : (after + 1) * 3 * CAP]
        value = t[:CAP] + t[CAP : 2 * CAP] + t[2 * CAP :]
        value = jnp.sum(jnp.where(chosen, value, 0.0), axis=0, keepdims=True)
        for b in range(blocks):
            out_ref[after, b : b + 1, :] = value[:, b * LANES : (b + 1) * LANES]

    returned.wait_send()
    sent = pltpu.make_async_remote_copy(
        src_ref=outgoing.at[0, pl.ds(0, PER - 1)],
        dst_ref=outgoing.at[0, pl.ds(0, PER - 1)],
        send_sem=send_sem,
        recv_sem=recv_sem.at[0],
        device_id=partner,
        device_id_type=MESH,
    )
    sent.wait_send()
    pltpu.make_async_remote_copy(
        src_ref=outgoing.at[pl.ds(1, PHASES - 1)],
        dst_ref=outgoing.at[pl.ds(1, PHASES - 1)],
        send_sem=send_sem,
        recv_sem=recv_sem.at[0],
        device_id=partner,
        device_id_type=MESH,
    ).wait_send()
    for t in range(PHASES):
        forward(t).wait_send()


def part(both_ref, first_ref, second_ref):
    first_ref[...] = both_ref[0]
    second_ref[...] = both_ref[1]


def body(embeddings, cluster_ids):
    anywhere = pl.BlockSpec(memory_space=pl.ANY)
    out = pl.pallas_call(
        kernel,
        out_shape=pltpu.VMEM((2, ROWS // LANES, LANES), jnp.float32),
        in_specs=[anywhere, anywhere],
        out_specs=pl.BlockSpec(memory_space=pltpu.VMEM),
        scratch_shapes=[
            pltpu.VMEM((ROWS, WIDTH), jnp.bfloat16),
            pltpu.VMEM((1, ROWS), jnp.int32),
            pltpu.VMEM((ROWS, WIDTH), jnp.bfloat16),
            pltpu.VMEM((PHASES, PER, CAP, WIDTH), jnp.bfloat16),
            pltpu.VMEM((PHASES, PER, CAP, WIDTH), jnp.bfloat16),
            pltpu.VMEM((PHASES, PER, CAP, WIDTH), jnp.bfloat16),
            pltpu.VMEM((2, PHASES, BLOCK, LANES), jnp.float32),
            pltpu.VMEM((PHASES, 2, 8, BLOCK), jnp.float32),
            pltpu.VMEM((PHASES * 2, 1, BLOCK), jnp.float32),
            pltpu.VMEM((2, PHASES, BLOCK, LANES), jnp.float32),
            pltpu.VMEM((2, 2, CHIPS, BLOCK), jnp.float32),
            pltpu.VMEM((CHIPS, LANES), jnp.int32),
            pltpu.VMEM((16, 2, LANES), jnp.float32),
            pltpu.VMEM((CHIPS, 2, LANES), jnp.float32),
            pltpu.VMEM((2, LANES, CHIPS), jnp.float32),
            pltpu.VMEM((CHIPS, ROWS), jnp.bfloat16),
            pltpu.VMEM((1, ROWS), jnp.int32),
            pltpu.VMEM((1, ROWS), jnp.int32),
            pltpu.VMEM((CHIPS, LANES), jnp.int32),
            pltpu.SemaphoreType.DMA,
            pltpu.SemaphoreType.DMA,
            pltpu.SemaphoreType.DMA,
            pltpu.SemaphoreType.DMA,
            pltpu.SemaphoreType.DMA((PHASES,)),
            pltpu.SemaphoreType.DMA((PHASES,)),
            pltpu.SemaphoreType.DMA((PHASES,)),
            pltpu.SemaphoreType.DMA,
            pltpu.SemaphoreType.DMA,
        ],
        compiler_params=pltpu.CompilerParams(
            collective_id=0, has_side_effects=True, vmem_limit_bytes=56 << 20
        ),
        cost_estimate=pl.CostEstimate(
            flops=2 * (2048 * 3072 + 2048 * 1024) * WIDTH, bytes_accessed=2 << 20, transcendentals=ROWS
        ),
    )(embeddings, cluster_ids.reshape(1, ROWS))
    line = jax.ShapeDtypeStruct((ROWS // LANES, LANES), jnp.float32)
    first, second = pl.pallas_call(
        part,
        out_shape=(line, line),
        in_specs=[pl.BlockSpec(memory_space=pltpu.VMEM)],
        out_specs=[pl.BlockSpec(memory_space=pltpu.VMEM)] * 2,
    )(pltpu.with_memory_space_constraint(out, pltpu.VMEM))
    return (first.reshape(ROWS), second.reshape(ROWS))


def solution(mesh):
    placed = (P(("files", "clus"), None), P(("files", "clus"), None))
    return jax.shard_map(
        body,
        mesh=mesh,
        in_specs=placed,
        out_specs=(P(("files", "clus")), P(("files", "clus"))),
        check_vma=False,
    )
```

```python
import jax
import jax.numpy as jnp
from jax import lax
from jax.experimental import pallas as pl
from jax.experimental.pallas import tpu as pltpu
from jax.sharding import PartitionSpec as P

MESH = pl.DeviceIdType.MESH
CHIPS = 64
CAP = 32
WIDTH = 512
ROWS = 1024
LANES = 128
PHASES = 8
PER = CHIPS // PHASES
BLOCK = PER * CAP


COSETS = (0, 7, 6, 5, 4, 3, 2, 1)


def offsets(t, j):
    a = -j % 4
    coset = COSETS[t]
    return (a + coset % 4) % 4, (a + 2 * (j // 4) + coset // 4) % 4, a


EMPTY = 2.0
NT = (((1,), (1,)), ((), ()))


def hops(offset):
    return sum(min(d, 4 - d) for d in offset)


FAR_FIRST = [sorted(range(PER), key=lambda j: -hops(offsets(t, j))) for t in range(PHASES)]


def kernel(
    emb_ref, lab_ref, out_ref,
    raw, lab, unit, outgoing, own, other, acc, cacc, bias_l, bias_s, masks, orders, res, ret, turned,
    onehot, rank_s, key_s, count_s,
    raw_sem, lab_sem, self_sem, send_sem, recv_sem, fwd_send, fwd_recv, ret_send, ret_recv,
):
    load = pltpu.make_async_copy(emb_ref, raw, raw_sem)
    load.start()
    load_lab = pltpu.make_async_copy(lab_ref, lab, lab_sem)
    load_lab.start()

    files, clus = lax.axis_index("files"), lax.axis_index("clus")
    z, y = lax.div(files, 4), lax.rem(files, 4)
    x, core = lax.div(clus, 2), lax.rem(clus, 2)
    here = x * 16 + files

    def wrap(v):
        return jnp.where(v >= 4, v - 4, v)

    zs, ys, xs = [[wrap(v + d) for d in range(4)] for v in (z, y, x)]
    partner = (files, clus + 1 - 2 * core)

    def target(t, j):
        dz, dy, dx = offsets(t, j)
        return (zs[dz] * 4 + ys[dy], xs[dx] * 2 + core)

    barrier = pltpu.get_barrier_semaphore()
    everyone = [(t, j) for t in range(PHASES) for j in range(PER)]
    for t, j in sorted(everyone, key=lambda tj: -hops(offsets(*tj))):
        to = target(t, j) if t or j else partner
        pl.semaphore_signal(barrier, inc=1, device_id=to, device_id_type=MESH)

    cluster = lax.broadcasted_iota(jnp.int32, (CHIPS, LANES), 0)
    blocks = ROWS // LANES
    earlier = jnp.where(
        lax.broadcasted_iota(jnp.int32, (LANES, LANES), 0)
        < lax.broadcasted_iota(jnp.int32, (LANES, LANES), 1),
        1.0,
        0.0,
    ).astype(jnp.bfloat16)
    load_lab.wait()
    labels = lab[...]
    labels = labels % 4 * 16 + labels // 4
    hot = [
        jnp.where(labels[:, b * LANES : (b + 1) * LANES] == cluster, 1.0, 0.0) for b in range(blocks)
    ]
    within = jnp.dot(
        jnp.concatenate(hot, axis=0).astype(jnp.bfloat16), earlier, preferred_element_type=jnp.float32
    )
    carry = jnp.zeros((CHIPS, 1), jnp.float32)
    for b in range(blocks):
        lanes = slice(b * LANES, (b + 1) * LANES)
        rank = jnp.sum(
            hot[b] * (within[b * CHIPS : (b + 1) * CHIPS] + carry), axis=0, keepdims=True
        ).astype(jnp.int32)
        rank_s[:, lanes] = rank
        key_s[:, lanes] = labels[:, lanes] * CAP + rank
        onehot[:, lanes] = hot[b].astype(jnp.bfloat16)
        carry = carry + jnp.sum(hot[b], axis=1, keepdims=True)
    count_s[...] = jnp.broadcast_to(carry, (CHIPS, LANES)).astype(jnp.int32)

    load.wait()
    for i in range(4):
        rows = slice(i * (ROWS // 4), (i + 1) * (ROWS // 4))
        e = raw[rows, :].astype(jnp.float32)
        squares = jnp.sum(e * e, axis=1, keepdims=True) + 1e-06
        unit[rows, :] = (e * lax.rsqrt(squares)).astype(jnp.bfloat16)

    def send(t, j):
        return pltpu.make_async_remote_copy(
            src_ref=outgoing.at[t, j],
            dst_ref=own.at[t, j],
            send_sem=send_sem,
            recv_sem=recv_sem.at[t],
            device_id=target(t, j),
            device_id_type=MESH,
        )

    keep = pltpu.make_async_copy(outgoing.at[0, 0], own.at[0, 0], self_sem)

    def pack(t):
        key = key_s[...]
        slot = lax.broadcasted_iota(jnp.int32, (CAP, ROWS), 0)
        row = lax.broadcasted_iota(jnp.int32, (CAP, LANES), 0)
        lane = lax.broadcasted_iota(jnp.int32, (CAP, LANES), 1)
        picks, holes = [], []
        for j in range(PER):
            dz, dy, dx = offsets(t, j)
            c = xs[dx] * 16 + zs[dz] * 4 + ys[dy]
            picks.append(jnp.where(key - c * CAP == slot, 1.0, 0.0).astype(jnp.bfloat16))
            holes.append((row >= count_s[pl.ds(c, 1), :]) & (lane == 0))
        rows = jnp.dot(jnp.concatenate(picks, axis=0), unit[...], preferred_element_type=jnp.float32)
        for j in range(PER):
            part = rows[j * CAP : (j + 1) * CAP]
            outgoing[t, j, :, :LANES] = jnp.where(holes[j], EMPTY, part[:, :LANES]).astype(jnp.bfloat16)
            outgoing[t, j, :, LANES:] = part[:, LANES:].astype(jnp.bfloat16)

    for t in range(PHASES):
        pack(t)
        if t == 0:
            pl.semaphore_wait(barrier, CHIPS)
            keep.start()
        for j in FAR_FIRST[t]:
            if t or j:
                send(t, j).start()

    def chip_order(coset, j):
        a = -j % 4
        sz = (z - a - coset % 4) % 4
        sy = (y - a - 2 * (j // 4) - coset // 4) % 4
        return sz * 16 + sy * 4 + (x + j) % 4

    i = lax.broadcasted_iota(jnp.int32, (PER, LANES), 0)
    for t in range(PHASES):
        orders[t * PER : (t + 1) * PER, :] = chip_order(COSETS[t], i)
    lane_j = lax.broadcasted_iota(jnp.int32, (1, BLOCK), 1) // CAP
    row_i = lax.broadcasted_iota(jnp.int32, (BLOCK, LANES), 0)

    def rows_of(ref, first, last):
        return ref[first:last].reshape((last - first) * BLOCK, WIDTH)

    def product(a, b):
        return lax.dot_general(a, b, NT, preferred_element_type=jnp.float32)

    def set_bias(ref, t, side):
        head = ref[t, :, :, :LANES].reshape(BLOCK, LANES).astype(jnp.float32)
        mark = jnp.broadcast_to(jnp.where(head[:, 0:1] > 1.5, -4.0, 0.0), (BLOCK, LANES))
        bias_s[side, t] = mark
        bias_l[t * 2 + side] = jnp.transpose(mark)[0:1, :]

        if t:
            columns = chip_order(COSETS[t], lane_j)
            rows = orders[: t * PER, 0:1]
            masks[side, 0, : t * PER, :] = jnp.where(columns < rows, bias_l[t * 2 + side], -4.0)
            masks[side, 1, : t * PER, :] = jnp.where(columns > rows, bias_l[t * 2 + side], -4.0)

    def halves(part):
        return jnp.maximum(part[:, :LANES], part[:, LANES:])

    def maxima(similar, t, side, row_side, rowwise, best):
        for i in range(t * PER):
            u, at = i // PER, slice(i % PER * CAP, (i % PER + 1) * CAP)
            part = similar[i * CAP : (i + 1) * CAP]
            if best is not None:
                mark = bias_s[row_side, u, at, :]
                part = jnp.concatenate([part[:, :LANES] + mark, part[:, LANES:] + mark], axis=1)
            for after in range(2):
                kept = part + masks[side, after, i : i + 1, :]
                if rowwise:
                    acc[after, u, at, :] = jnp.maximum(acc[after, u, at, :], halves(kept))
                if best is not None:
                    high = jnp.max(kept.reshape(CAP // 8, 8, BLOCK), axis=0)
                    best[1 - after] = jnp.maximum(best[1 - after], high)

    def diagonal(t, side):
        similar = product(rows_of(own, t, t + 1), rows_of(other if side else own, t, t + 1))
        similar = similar + bias_l[t * 2 + side]
        lane = lax.broadcasted_iota(jnp.int32, (1, BLOCK), 1)
        mine = (chip_order(COSETS[t], row_i // CAP) * (2 * CAP) + row_i % CAP)[:, 0:1]
        theirs = chip_order(COSETS[t], lane_j) * (2 * CAP) + lane % CAP
        if side:
            theirs = theirs + (1 - 2 * core) * CAP
        for after in range(2):
            mask = theirs > mine if after else theirs < mine
            part = halves(jnp.where(mask, similar, -1.0))
            if side:
                acc[after, t] = jnp.maximum(acc[after, t], part)
            else:
                acc[after, t] = jnp.maximum(part, -1.0)

    def forward(t):
        return pltpu.make_async_remote_copy(
            src_ref=own.at[t],
            dst_ref=other.at[t],
            send_sem=fwd_send.at[t],
            recv_sem=fwd_recv.at[t],
            device_id=partner,
            device_id_type=MESH,
        )

    def arrived(t):
        blocks_of = own.at[t] if t else own.at[t, pl.ds(0, PER - 1)]
        pltpu.make_async_remote_copy(
            src_ref=blocks_of,
            dst_ref=blocks_of,
            send_sem=send_sem,
            recv_sem=recv_sem.at[t],
            device_id=partner,
            device_id_type=MESH,
        ).wait_recv()

    for t in range(PHASES):
        if t == 0:
            keep.wait()
            arrived(0)
            forward(0).start()
        set_bias(own, t, 0)
        mine = rows_of(own, t, t + 1)
        best = [jnp.full((8, BLOCK), -1.0, jnp.float32)] * 2
        if t:
            maxima(product(rows_of(own, 0, t), mine), t, 0, 0, True, best)
            maxima(product(rows_of(other, 0, t), mine), t, 0, 1, False, best)
        for after in range(2):
            cacc[t, after] = best[after]
        diagonal(t, 0)
        forward(t).wait_recv()
        if t + 1 < PHASES:
            arrived(t + 1)
            forward(t + 1).start()
        set_bias(other, t, 1)
        if t:
            maxima(product(rows_of(own, 0, t), rows_of(other, t, t + 1)), t, 1, 0, True, None)
        diagonal(t, 1)

    for t in range(PHASES):
        for after in range(2):
            best = jnp.max(jnp.transpose(acc[after, t]), axis=0, keepdims=True)
            best = jnp.maximum(best, jnp.max(cacc[t, after], axis=0, keepdims=True))
            for half in range(2):
                line = best[:, half * LANES : (half + 1) * LANES]
                res[t * 2 + half, after : after + 1, :] = pltpu.roll(line, x * CAP, 1)
    line_of = {offsets(t, j): t * 2 + j // 4 for t in range(PHASES) for j in range(PER)}
    back = [(dz, dy, dx) for dz in range(4) for dy in range(4) for dx in range(4)]
    for dz, dy, dx in sorted(back, key=hops, reverse=True)[:-1]:
        pltpu.make_async_remote_copy(
            src_ref=res.at[line_of[dz, dy, dx]],
            dst_ref=ret.at[here],
            send_sem=ret_send,
            recv_sem=ret_recv,
            device_id=(zs[-dz % 4] * 4 + ys[-dy % 4], xs[-dx % 4] * 2 + core),
            device_id_type=MESH,
        ).start()
    ret[here] = res[0]

    returned = pltpu.make_async_remote_copy(
        src_ref=ret.at[pl.ds(0, CHIPS - 1)],
        dst_ref=ret.at[pl.ds(0, CHIPS - 1)],
        send_sem=ret_send,
        recv_sem=ret_recv,
        device_id=partner,
        device_id_type=MESH,
    )
    returned.wait_recv()

    for after in range(2):
        turned[after] = jnp.transpose(ret[:, after, :])
    pieces = []
    for after in range(2):
        rest = turned[after, pl.ds(pl.multiple_of(x * CAP, CAP), CAP), :]
        for _ in range(3):
            piece = rest.astype(jnp.bfloat16)
            pieces.append(piece)
            rest = rest - piece.astype(jnp.float32)
    table = jnp.dot(
        jnp.concatenate(pieces, axis=0), onehot[...], preferred_element_type=jnp.float32
    )
    chosen = lax.broadcasted_iota(jnp.int32, (CAP, ROWS), 0) == rank_s[...]
    for after in range(2):
        t = table[after * 3 * CAP : (after + 1) * 3 * CAP]
        value = t[:CAP] + t[CAP : 2 * CAP] + t[2 * CAP :]
        value = jnp.sum(jnp.where(chosen, value, 0.0), axis=0, keepdims=True)
        for b in range(blocks):
            out_ref[after, b : b + 1, :] = value[:, b * LANES : (b + 1) * LANES]

    returned.wait_send()
    sent = pltpu.make_async_remote_copy(
        src_ref=outgoing.at[0, pl.ds(0, PER - 1)],
        dst_ref=outgoing.at[0, pl.ds(0, PER - 1)],
        send_sem=send_sem,
        recv_sem=recv_sem.at[0],
        device_id=partner,
        device_id_type=MESH,
    )
    sent.wait_send()
    pltpu.make_async_remote_copy(
        src_ref=outgoing.at[pl.ds(1, PHASES - 1)],
        dst_ref=outgoing.at[pl.ds(1, PHASES - 1)],
        send_sem=send_sem,
        recv_sem=recv_sem.at[0],
        device_id=partner,
        device_id_type=MESH,
    ).wait_send()
    for t in range(PHASES):
        forward(t).wait_send()


def part(both_ref, first_ref, second_ref):
    first_ref[...] = both_ref[0]
    second_ref[...] = both_ref[1]


def body(embeddings, cluster_ids):
    anywhere = pl.BlockSpec(memory_space=pl.ANY)
    out = pl.pallas_call(
        kernel,
        out_shape=pltpu.VMEM((2, ROWS // LANES, LANES), jnp.float32),
        in_specs=[anywhere, anywhere],
        out_specs=pl.BlockSpec(memory_space=pltpu.VMEM),
        scratch_shapes=[
            pltpu.VMEM((ROWS, WIDTH), jnp.bfloat16),
            pltpu.VMEM((1, ROWS), jnp.int32),
            pltpu.VMEM((ROWS, WIDTH), jnp.bfloat16),
            pltpu.VMEM((PHASES, PER, CAP, WIDTH), jnp.bfloat16),
            pltpu.VMEM((PHASES, PER, CAP, WIDTH), jnp.bfloat16),
            pltpu.VMEM((PHASES, PER, CAP, WIDTH), jnp.bfloat16),
            pltpu.VMEM((2, PHASES, BLOCK, LANES), jnp.float32),
            pltpu.VMEM((PHASES, 2, 8, BLOCK), jnp.float32),
            pltpu.VMEM((PHASES * 2, 1, BLOCK), jnp.float32),
            pltpu.VMEM((2, PHASES, BLOCK, LANES), jnp.float32),
            pltpu.VMEM((2, 2, CHIPS, BLOCK), jnp.float32),
            pltpu.VMEM((CHIPS, LANES), jnp.int32),
            pltpu.VMEM((16, 2, LANES), jnp.float32),
            pltpu.VMEM((CHIPS, 2, LANES), jnp.float32),
            pltpu.VMEM((2, LANES, CHIPS), jnp.float32),
            pltpu.VMEM((CHIPS, ROWS), jnp.bfloat16),
            pltpu.VMEM((1, ROWS), jnp.int32),
            pltpu.VMEM((1, ROWS), jnp.int32),
            pltpu.VMEM((CHIPS, LANES), jnp.int32),
            pltpu.SemaphoreType.DMA,
            pltpu.SemaphoreType.DMA,
            pltpu.SemaphoreType.DMA,
            pltpu.SemaphoreType.DMA,
            pltpu.SemaphoreType.DMA((PHASES,)),
            pltpu.SemaphoreType.DMA((PHASES,)),
            pltpu.SemaphoreType.DMA((PHASES,)),
            pltpu.SemaphoreType.DMA,
            pltpu.SemaphoreType.DMA,
        ],
        compiler_params=pltpu.CompilerParams(
            collective_id=0, has_side_effects=True, vmem_limit_bytes=56 << 20
        ),
        cost_estimate=pl.CostEstimate(
            flops=2 * (2048 * 3072 + 2048 * 1024) * WIDTH, bytes_accessed=2 << 20, transcendentals=ROWS
        ),
    )(embeddings, cluster_ids.reshape(1, ROWS))
    line = jax.ShapeDtypeStruct((ROWS // LANES, LANES), jnp.float32)
    first, second = pl.pallas_call(
        part,
        out_shape=(line, line),
        in_specs=[pl.BlockSpec(memory_space=pltpu.VMEM)],
        out_specs=[pl.BlockSpec(memory_space=pltpu.VMEM)] * 2,
    )(pltpu.with_memory_space_constraint(out, pltpu.VMEM))
    return (first.reshape(ROWS), second.reshape(ROWS))


def solution(mesh):
    placed = (P(("files", "clus"), None), P(("files", "clus"), None))
    return jax.shard_map(
        body,
        mesh=mesh,
        in_specs=placed,
        out_specs=(P(("files", "clus")), P(("files", "clus"))),
        check_vma=False,
    )
```
